512 devices in a mesh: ctx: 128 (over z, y, core), head: 4 (over x).
Axes of the slice: x: 4, y: 4, z: 16, core: 2. Of those that a mesh axis runs over, the one named last changes fastest.
Arguments:
- queries: bfloat16 [49152, 24, 128], P('ctx', 'head'), may hold values from -35 to 35
- keys: bfloat16 [49152, 24, 128], P('ctx', 'head'), may hold values from -35 to 35
- values: bfloat16 [49152, 24, 128], P('ctx', 'head'), may hold values from -6 to 6
- out_grads: bfloat16 [49152, 24, 128], P('ctx', 'head'), may hold values from -6 to 6
- query_gain: float32 [24, 128], P('head'), may hold values from 0.5 to 1.5
- key_gain: float32 [24, 128], P('head'), may hold values from 0.5 to 1.5
- block_lengths: int32 [256], replicated, may hold values from 1 to 384, 49152 in all
Outputs:
- query_grad: bfloat16 [49152, 24, 128], P('ctx', 'head')
- key_grad: bfloat16 [49152, 24, 128], P('ctx', 'head')
- value_grad: bfloat16 [49152, 24, 128], P('ctx', 'head')
The draws below stay inside these ranges and needn't reach their ends.
Inputs may be any that keep to these rules, and one draw needn't show every extreme that they name: `block_lengths`: the lengths sum to 49152, and the longest block has exactly 384 tokens.
All inputs are finite; a program needn't handle non-finite values.
Results may differ from the reference program's by a relative error of at most 0.012.
Values may be sent and summed in bfloat16 or wider, within the bound.
A program may use at most 64 MiB of HBM per device.

```python
import math
import jax
import jax.numpy as jnp
import numpy as np
from jax import lax

HEADS = 24
DH = 128
TOK_DEV = 384
MOST = 384
TOKENS = 49152
NBLOCK = 256


def draw_queries(key, part):
    key = jax.random.fold_in(key, 5)
    result = jnp.clip(jax.random.normal(key, (TOKENS, HEADS, DH), jnp.float32), -4.0, 4.0)
    return result.astype(jnp.bfloat16)


def draw_keys(key, part):
    key = jax.random.fold_in(key, 7)
    result = jnp.clip(jax.random.normal(key, (TOKENS, HEADS, DH), jnp.float32), -4.0, 4.0)
    return result.astype(jnp.bfloat16)


def level_of(own_key, shape, pieces, least, largest):
    gain = 1.0
    for dim, blocks in pieces:
        heights = jax.random.uniform(jax.random.fold_in(jax.random.fold_in(own_key, 6), dim), (blocks,), jnp.float32, least / len(pieces), largest / len(pieces))
        gain = gain * jnp.repeat(jnp.exp(heights), shape[dim] // blocks).reshape((-1,) + (1,) * (len(shape) - 1 - dim))
    return gain


def profile(count, total, limit, lean):
    loads = [(1 << 20) // math.isqrt(grade ** lean) + 1 for grade in range(2, count + 1)]
    spare, holding = total - limit - (count - 1), [1] * (count - 1)
    while spare > 0:
        free = [i for i in range(count - 1) if holding[i] < limit]
        pool, budget = sum([loads[i] for i in free]), spare
        for i in free:
            extra = min(limit - holding[i], max(1, budget * loads[i] // pool), spare)
            holding[i] = holding[i] + extra
            spare = spare - extra
    return np.array([limit] + holding)


def uneven(rng, count, total, reach, slope):
    if count == 2:
        one = jax.random.randint(rng, (), max(1, total - reach), min(reach, total - 1) + 1)
        return jnp.stack([one, total - one])
    tallies = jnp.asarray(profile(count, total, reach, slope), jnp.int32)
    pairs = (count - 1) // 2
    donor, sink = tallies[1:1 + 2 * pairs:2], tallies[2:2 + 2 * pairs:2]
    slack = jnp.minimum(donor - 1, reach - sink)
    passed = jax.random.randint(jax.random.fold_in(rng, 1), (pairs,), 0, 1 << 20) % (slack + 1)
    tallies = tallies.at[1:1 + 2 * pairs:2].set(donor - passed).at[2:2 + 2 * pairs:2].set(sink + passed)
    return tallies[jax.random.permutation(jax.random.fold_in(rng, 2), count)]


def gaussian(own_key, extent, spread, most, shards=(), kind=jnp.bfloat16):
    level = level_of(own_key, extent, shards, -0.22, 0.18) if shards else 1.0
    drawn = jax.random.normal(own_key, extent, jnp.float32) * spread * level
    return jnp.minimum(jnp.maximum(drawn, -most), most).astype(kind)


def setup_inputs(seed: int = 0) -> dict:
    streams_of = jax.random.split(jax.random.key(seed), 8)
    queries = draw_queries(jax.random.fold_in(streams_of[7], 71), 0)
    keys = draw_keys(jax.random.fold_in(streams_of[7], 71), 0)
    values = gaussian(streams_of[2], (TOKENS, HEADS, DH), 1.0, 6.0, ((0, 128), (1, 4)))
    out_grads = gaussian(streams_of[3], (TOKENS, HEADS, DH), 1.0, 6.0, ((0, 128), (1, 4)))
    query_gain = jnp.clip(1.0 + 0.1 * jax.random.normal(streams_of[4], (HEADS, DH), jnp.float32), 0.5, 1.5)
    key_gain = jnp.clip(1.0 + 0.1 * jax.random.normal(streams_of[5], (HEADS, DH), jnp.float32), 0.5, 1.5)
    block_lengths = uneven(streams_of[6], NBLOCK, TOKENS, MOST, 2).astype(jnp.int32)
    return {"queries": queries, "keys": keys, "values": values, "out_grads": out_grads, "query_gain": query_gain, "key_gain": key_gain, "block_lengths": block_lengths}


masked_score = -1e+30
norm_eps = 1e-06

def block_index(positions, block_ends):
    return lax.optimization_barrier(jnp.sum((block_ends[None, :] <= positions[:, None]).astype(jnp.int32), axis=1))

def visible(query_pos, key_pos, block_ends, all_tokens):
    query_block = block_index(query_pos, block_ends)
    key_block = block_index(key_pos, block_ends)
    query_live = (query_pos >= 0) & (query_pos < all_tokens)
    key_live = (key_pos >= 0) & (key_pos < all_tokens)
    inside = query_live[:, None] & key_live[None, :]
    return inside & (key_block[None, :] <= query_block[:, None]) & (key_block[None, :] >= query_block[:, None] - 1)

def dense_head(query_h, grad_h, key_h, value_h, allowed, score_scale):
    scores = jnp.where(allowed, jnp.dot(query_h, key_h.T, preferred_element_type=jnp.float32) * score_scale, masked_score)
    row_max = lax.optimization_barrier(jnp.max(scores, axis=1, keepdims=True))
    weights = jnp.where(allowed, jnp.exp(scores - row_max), 0.0)
    probs = weights / lax.optimization_barrier(jnp.sum(weights, axis=1, keepdims=True))
    grad_probs = jnp.dot(grad_h, value_h.T, preferred_element_type=jnp.float32)
    delta = lax.optimization_barrier(jnp.sum(probs * grad_probs, axis=1, keepdims=True))
    score_grad = (probs * (grad_probs - delta)).astype(jnp.bfloat16)
    probs_low = probs.astype(jnp.bfloat16)
    query_part = jnp.dot(score_grad, key_h, preferred_element_type=jnp.float32) * score_scale
    key_part = jnp.dot(score_grad.T, query_h, preferred_element_type=jnp.float32) * score_scale
    value_part = jnp.dot(probs_low.T, grad_h, preferred_element_type=jnp.float32)
    return (query_part, key_part, value_part)

def norm_forward(source, norm_gain):
    source_f = source.astype(jnp.float32)
    inv_rms = lax.rsqrt(lax.optimization_barrier(jnp.mean(source_f * source_f, axis=(1, 2))) + norm_eps)
    return (inv_rms, (source_f * inv_rms[:, None, None] * norm_gain[None]).astype(jnp.bfloat16))

def norm_backward(source, norm_gain, inv_rms, upstream):
    source_f = source.astype(jnp.float32)
    scaled = upstream * norm_gain[None]
    products = lax.optimization_barrier(jnp.mean(scaled * source_f, axis=(1, 2)))
    result = inv_rms[:, None, None] * scaled - source_f * (inv_rms ** 3 * products)[:, None, None]
    return result.astype(jnp.bfloat16)

def reference(queries, keys, values, out_grads, query_gain, key_gain, block_lengths):
    all_tokens = queries.shape[0]
    width = TOK_DEV
    span = 4 * width
    score_scale = DH ** (-0.5)
    block_ends = jnp.cumsum(block_lengths).astype(jnp.int32)
    inv_q, query_norm = norm_forward(queries, query_gain)
    inv_k, key_norm = norm_forward(keys, key_gain)
    query_heads = jnp.moveaxis(query_norm, 1, 0)
    grad_heads = jnp.moveaxis(out_grads, 1, 0)
    key_heads = jnp.pad(jnp.moveaxis(key_norm, 1, 0), ((0, 0), (2 * width, width), (0, 0)))
    value_heads = jnp.pad(jnp.moveaxis(values, 1, 0), ((0, 0), (2 * width, width), (0, 0)))
    blocks_count = all_tokens // width

    def per_head(operands):
        query_h, grad_h, key_pad, value_pad = operands

        def per_block(carry, block_number):
            key_acc, value_acc = carry
            start = (block_number * width).astype(jnp.int32)
            query_rows = lax.dynamic_slice_in_dim(query_h, start, width, 0)
            grad_rows = lax.dynamic_slice_in_dim(grad_h, start, width, 0)
            key_rows = lax.dynamic_slice_in_dim(key_pad, start, span, 0)
            value_rows = lax.dynamic_slice_in_dim(value_pad, start, span, 0)
            query_pos = start + jnp.arange(width, dtype=jnp.int32)
            key_pos = start - 2 * width + jnp.arange(span, dtype=jnp.int32)
            allowed = visible(query_pos, key_pos, block_ends, all_tokens)
            query_part, key_part, value_part = dense_head(query_rows, grad_rows, key_rows, value_rows, allowed, score_scale)
            key_acc = lax.dynamic_update_slice_in_dim(key_acc, lax.dynamic_slice_in_dim(key_acc, start, span, 0) + key_part, start, 0)
            value_acc = lax.dynamic_update_slice_in_dim(value_acc, lax.dynamic_slice_in_dim(value_acc, start, span, 0) + value_part, start, 0)
            return ((key_acc, value_acc), query_part)
        zeros = jnp.zeros((all_tokens + 3 * width, DH), jnp.float32)
        (key_acc, value_acc), query_blocks = lax.scan(per_block, (zeros, zeros), jnp.arange(blocks_count, dtype=jnp.int32))
        return (query_blocks.reshape(all_tokens, DH), key_acc[2 * width:2 * width + all_tokens], value_acc[2 * width:2 * width + all_tokens])
    query_parts, key_parts, value_parts = lax.map(per_head, (query_heads, grad_heads, key_heads, value_heads))
    query_norm_grad = jnp.moveaxis(query_parts, 0, 1)
    key_norm_grad = jnp.moveaxis(key_parts, 0, 1)
    value_grad = jnp.moveaxis(value_parts, 0, 1).astype(jnp.bfloat16)
    query_grad = norm_backward(queries, query_gain, inv_q, query_norm_grad)
    key_grad = norm_backward(keys, key_gain, inv_k, key_norm_grad)
    return (query_grad, key_grad, value_grad)
```

```python
import functools

import jax
import jax.numpy as jnp
from jax import lax
from jax.experimental import pallas as pl
from jax.experimental.pallas import tpu as pltpu
from jax.sharding import PartitionSpec as P

MESH = pl.DeviceIdType.MESH
norm_eps = 1e-06
hidden = -1e30
BF = jnp.bfloat16
F32 = jnp.float32

TOK = 384
PAIR = 2 * TOK
SPAN = 5 * TOK
LOC = 6
HALF = 3
DH = 128
QT = 256
NQ = PAIR // QT
WIN = 1408
KC = 128
NK = WIN // KC


def dot(a, b):
    return jnp.dot(a, b, preferred_element_type=F32)


def lanes_sum_row(x):
    return jnp.sum(x.T, axis=0, keepdims=True)


def row_to_full(row):
    return jnp.broadcast_to(row, (DH, row.shape[1])).T


def body(
    nctx, nx,
    q_hbm, k_hbm, v_hbm, d_hbm, qg_ref, kg_ref, len_ref,
    oq_ref, ok_ref, ov_ref,
    qraw, kraw, qn, kn, kw, vw, qw, dw,
    invq, invk, st_a, st_b, sd_a, sd_b,
    bias, sbuf, pbuf, kt, dk_acc, dv_acc,
    dk_snd, dv_snd, dq_snd, rn, rp, rs, gq, gk,
    lsem, s_fn, r_fn, s_fp, r_fp, s_sib, r_sib, s_x, r_x, s_rp, r_rn, s_rn, r_rp, s_rs, r_rs,
):
    me = lax.axis_index("ctx")
    x = lax.axis_index("head")
    core = lax.rem(me, 2)
    chip = me // 2
    chips = nctx // 2
    has_prev = chip > 0
    has_next = chip < chips - 1
    other = 1 - core
    features = float(nx * LOC * DH)
    scale = DH ** -0.5
    log2e = 1.4426950408889634
    sib_dev = (2 * chip + other, x)
    x_devs = [(me, lax.rem(x + d, nx)) for d in range(1, nx)]

    def next_dev(kk):
        return (2 * chip + 2 + kk, x)

    def prev_dev(kk):
        return (2 * chip - 2 + kk, x)

    def remote(src, dst, ss, rs_, dev):
        return pltpu.make_async_remote_copy(
            src_ref=src, dst_ref=dst, send_sem=ss, recv_sem=rs_, device_id=dev, device_id_type=MESH
        )

    bar = pltpu.get_barrier_semaphore()

    @pl.when(has_next)
    def _():
        for kk in range(2):
            pl.semaphore_signal(bar, inc=1, device_id=next_dev(kk), device_id_type=MESH)

    @pl.when(has_prev)
    def _():
        for kk in range(2):
            pl.semaphore_signal(bar, inc=1, device_id=prev_dev(kk), device_id_type=MESH)

    pl.semaphore_signal(bar, inc=1, device_id=sib_dev, device_id_type=MESH)
    for dev in x_devs:
        pl.semaphore_signal(bar, inc=1, device_id=dev, device_id_type=MESH)

    own = pl.ds(pl.multiple_of(core * TOK, TOK), TOK)
    own_win = pl.ds(pl.multiple_of(PAIR + core * TOK, TOK), TOK)
    own_heads = pl.ds(core * HALF, HALF)
    sib_heads = pl.ds(other * HALF, HALF)
    load_k = pltpu.make_async_copy(k_hbm, kraw, lsem.at[0])
    load_q = pltpu.make_async_copy(q_hbm, qraw, lsem.at[1])
    self_v = pltpu.make_async_copy(v_hbm.at[own_heads], vw.at[:, own_win], lsem.at[2])
    self_d = pltpu.make_async_copy(d_hbm.at[own_heads], dw.at[:, own], lsem.at[3])
    load_k.start()
    load_q.start()
    self_v.start()
    self_d.start()

    @pl.when(has_prev & has_next)
    def _():
        pl.semaphore_wait(bar, nx + 4)

    @pl.when(jnp.logical_not(has_prev & has_next))
    def _():
        pl.semaphore_wait(bar, nx + 2)

    def fwd_next(arr, h, kk):
        src = (v_hbm, kn)[arr].at[kk * HALF + h]
        dst = (vw, kw)[arr].at[h, own]
        return remote(src, dst, s_fn.at[arr, h, kk], r_fn.at[arr, h, core], next_dev(kk))

    def fwd_prev(arr, h, kk):
        src = (v_hbm, kn)[arr].at[kk * HALF + h]
        dst = (vw, kw)[arr].at[h, pl.ds(2 * PAIR, TOK)]
        return remote(src, dst, s_fp.at[arr, h, kk], r_fp.at[arr, h], prev_dev(kk))

    def fwd(arr, h):
        @pl.when(has_next)
        def _():
            for kk in range(2):
                fwd_next(arr, h, kk).start()

        @pl.when(has_prev & (core == 0))
        def _():
            for kk in range(2):
                fwd_prev(arr, h, kk).start()

    to_sib = [
        remote(v_hbm.at[sib_heads], vw.at[:, own_win], s_sib.at[0], r_sib.at[0], sib_dev),
        remote(d_hbm.at[sib_heads], dw.at[:, own], s_sib.at[1], r_sib.at[1], sib_dev),
        remote(kn.at[sib_heads], kw.at[:, own_win], s_sib.at[2], r_sib.at[2], sib_dev),
        remote(qn.at[sib_heads], qw.at[:, own], s_sib.at[3], r_sib.at[3], sib_dev),
    ]
    fwd(0, 0)
    to_sib[0].start()
    to_sib[1].start()

    def all_sum(rows, mine, theirs, rnd):
        mine[0:1, :] = rows[0]
        mine[1:2, :] = rows[1]
        copies = [
            remote(mine, theirs.at[d], s_x.at[rnd, d], r_x.at[rnd, d], x_devs[d]) for d in range(nx - 1)
        ]
        for c in copies:
            c.start()
        for c in copies:
            c.wait()
        total = mine[0:2, :]
        for d in range(nx - 1):
            total = total + theirs[d, 0:2, :]
        return total[0:1, :], total[1:2, :]

    def squares(ref):
        total = jnp.zeros((TOK, DH), F32)
        for g in range(LOC):
            v = ref[g].astype(F32)
            total = total + v * v
        return lanes_sum_row(total)

    load_q.wait()
    load_k.wait()
    mine = st_a
    mine[...] = jnp.zeros_like(mine)
    sum_q, sum_k = all_sum((squares(qraw), squares(kraw)), st_a, st_b, 0)
    invk[...] = row_to_full(lax.rsqrt(sum_k / features + norm_eps))
    invq[...] = row_to_full(lax.rsqrt(sum_q / features + norm_eps))
    for h in range(HALF):
        for kk in range(2):
            g = kk * HALF + h
            kn[g] = (kraw[g].astype(F32) * invk[...] * kg_ref[g : g + 1, :]).astype(BF)
        fwd(1, h)
        if h < HALF - 1:
            fwd(0, h + 1)
    to_sib[2].start()
    for g in range(LOC):
        qn[g] = (qraw[g].astype(F32) * invq[...] * qg_ref[g : g + 1, :]).astype(BF)
    to_sib[3].start()
    self_k = pltpu.make_async_copy(kn.at[own_heads], kw.at[:, own_win], lsem.at[4])
    self_q = pltpu.make_async_copy(qn.at[own_heads], qw.at[:, own], lsem.at[5])
    self_k.start()
    self_q.start()

    @pl.when(jnp.logical_not(has_prev))
    def _():
        for h in range(HALF):
            kw[h, 0:PAIR] = jnp.zeros((PAIR, DH), BF)
            vw[h, 0:PAIR] = jnp.zeros((PAIR, DH), BF)

    @pl.when(jnp.logical_not(has_next))
    def _():
        for h in range(HALF):
            kw[h, 2 * PAIR : SPAN] = jnp.zeros((TOK, DH), BF)
            vw[h, 2 * PAIR : SPAN] = jnp.zeros((TOK, DH), BF)
        rn[...] = jnp.zeros_like(rn)

    @pl.when(jnp.logical_not(has_prev & (core == 0)))
    def _():
        rp[...] = jnp.zeros_like(rp)

    nb = len_ref.shape[1]
    lens = len_ref[...].astype(F32)
    ri = lax.broadcasted_iota(jnp.int32, (nb, nb), 0)
    ci = lax.broadcasted_iota(jnp.int32, (nb, nb), 1)
    ends_col = jnp.sum(jnp.where(ci <= ri, lens, 0.0), axis=1, keepdims=True)
    start = chip * PAIR - PAIR
    pos = (start + lax.broadcasted_iota(jnp.int32, (1, SPAN), 1)).astype(F32)
    blocks = jnp.sum(jnp.where(ends_col <= pos, 1.0, 0.0), axis=0, keepdims=True)
    q_block = blocks[:, PAIR : 2 * PAIR]
    k_block = jnp.where(pos >= 0.0, blocks, -10.0)
    k_full = row_to_full(k_block)
    for t in range(NQ):
        kb = k_full[t * QT : t * QT + WIN]
        for c in range(QT // DH):
            qb = q_block[:, t * QT + c * DH : t * QT + (c + 1) * DH]
            seen = (kb <= qb) & (kb >= qb - 1.0)
            bias[t, :, c * DH : (c + 1) * DH] = jnp.where(seen, 0.0, hidden)

    self_v.wait()
    self_d.wait()
    self_k.wait()
    self_q.wait()
    for c in to_sib:
        c.wait_recv()

    def ret_prev(arr, h, kk):
        src = (dv_snd, dk_snd)[arr].at[h, pl.ds(kk * TOK, TOK)]
        dst = rn.at[arr, core * HALF + h]
        return remote(src, dst, s_rp.at[arr, h, kk], r_rn.at[arr, h, core], prev_dev(kk))

    def ret_next(arr, h):
        src = (dv_snd, dk_snd)[arr].at[h, pl.ds(2 * PAIR, TOK)]
        dst = rp.at[arr, core * HALF + h]
        return remote(src, dst, s_rn.at[arr, h], r_rp.at[arr, h, core], next_dev(0))

    def ret_sib(arr, h):
        if arr < 2:
            src = (dv_snd, dk_snd)[arr].at[h, pl.ds(pl.multiple_of(PAIR + other * TOK, TOK), TOK)]
        else:
            src = dq_snd.at[h, pl.ds(pl.multiple_of(other * TOK, TOK), TOK)]
        return remote(src, rs.at[arr, h], s_rs.at[arr, h], r_rs.at[arr, h], sib_dev)

    def tile(h, t):
        first = pl.multiple_of(t * QT, QT)
        q_rows = qw[h, pl.ds(first, QT)]
        d_rows = dw[h, pl.ds(first, QT)]
        q_t = q_rows.T
        d_t = d_rows.T

        def keys_at(j):
            return pl.ds(pl.multiple_of(first + j * KC, KC), KC)

        top = jnp.full((8, QT), -3e38, F32)
        for j in range(NK):
            s = dot(kw[h, keys_at(j)], q_t) + bias[t, j * KC : (j + 1) * KC]
            sbuf[j * KC : (j + 1) * KC] = s
            top = jnp.maximum(top, jnp.max(s.reshape(KC // 8, 8, QT), axis=0))
        top = jnp.max(top, axis=0, keepdims=True)
        total = jnp.zeros((8, QT), F32)
        delta = jnp.zeros((8, QT), F32)
        for j in range(NK):
            rows = slice(j * KC, (j + 1) * KC)
            p = jnp.exp2((sbuf[rows] - top) * (scale * log2e))
            dp = dot(vw[h, keys_at(j)], d_t)
            pbuf[rows] = p
            sbuf[rows] = dp
            total = total + jnp.sum(p.reshape(KC // 8, 8, QT), axis=0)
            delta = delta + jnp.sum((p * dp).reshape(KC // 8, 8, QT), axis=0)
        inverse = 1.0 / jnp.sum(total, axis=0, keepdims=True)
        delta = jnp.sum(delta, axis=0, keepdims=True) * inverse
        inv_full = row_to_full(inverse)
        q_r = (q_rows.astype(F32) * inv_full).astype(BF)
        d_r = (d_rows.astype(F32) * inv_full).astype(BF)
        dq_t = jnp.zeros((DH, QT), F32)
        for j in range(NK):
            rows = slice(j * KC, (j + 1) * KC)
            p = pbuf[rows]
            ds = (p * (sbuf[rows] - delta)).astype(BF)
            at = keys_at(j)
            dv_acc[at] = dv_acc[at] + dot(p.astype(BF), d_r)
            dk_acc[at] = dk_acc[at] + dot(ds, q_r)
            dq_t = dq_t + dot(kt[:, at], ds)
        dq_snd[h, pl.ds(first, QT)] = (dq_t * (inverse * scale)).T.astype(BF)

    def head(h, carry):
        @pl.when(has_prev)
        def _():
            for arr in range(2):
                for kk in range(2):
                    remote(
                        v_hbm.at[0], (vw, kw)[arr].at[h, pl.ds(kk * TOK, TOK)],
                        s_fn.at[arr, h, kk], r_fn.at[arr, h, kk], prev_dev(kk),
                    ).wait_recv()

        @pl.when(has_next)
        def _():
            for arr in range(2):
                remote(
                    v_hbm.at[0], (vw, kw)[arr].at[h, pl.ds(2 * PAIR, TOK)],
                    s_fp.at[arr, h, 0], r_fp.at[arr, h], next_dev(0),
                ).wait_recv()

        for j in range(SPAN // KC):
            kt[:, j * KC : (j + 1) * KC] = kw[h, j * KC : (j + 1) * KC].T
        dk_acc[...] = jnp.zeros_like(dk_acc)
        dv_acc[...] = jnp.zeros_like(dv_acc)
        lax.fori_loop(0, NQ, lambda t, c: (tile(h, t), c)[1], 0)
        dk_snd[h] = (dk_acc[...] * scale).astype(BF)
        dv_snd[h] = dv_acc[...].astype(BF)

        @pl.when(has_prev)
        def _():
            for arr in range(2):
                for kk in range(2):
                    ret_prev(arr, h, kk).start()

        @pl.when(has_next)
        def _():
            for arr in range(2):
                ret_next(arr, h).start()

        for arr in range(3):
            ret_sib(arr, h).start()
        return carry

    lax.fori_loop(0, HALF, head, 0)

    for arr in range(3):
        for h in range(HALF):
            ret_sib(arr, h).wait_recv()

    def parts(h, sib):
        g = (other if sib else core) * HALF + h
        if sib:
            return g, rs[2, h], rs[1, h], rs[0, h]
        return g, dq_snd[h, own], dk_snd[h, own_win], dv_snd[h, own_win]

    dots_q = jnp.zeros((TOK, DH), F32)
    for h in range(HALF):
        for sib in (False, True):
            g, pq, _, _ = parts(h, sib)
            up = pq.astype(F32) * qg_ref[pl.ds(g, 1), :]
            gq[g] = up
            dots_q = dots_q + up * qraw[g].astype(F32)

    @pl.when(has_next)
    def _():
        for h in range(HALF):
            for arr in range(2):
                for kk in range(2):
                    remote(
                        v_hbm.at[0], rn.at[arr, kk * HALF + h],
                        s_rp.at[arr, h, kk], r_rn.at[arr, h, kk], next_dev(kk),
                    ).wait_recv()

    @pl.when(has_prev & (core == 0))
    def _():
        for h in range(HALF):
            for arr in range(2):
                for kk in range(2):
                    remote(
                        v_hbm.at[0], rp.at[arr, kk * HALF + h],
                        s_rn.at[arr, h], r_rp.at[arr, h, kk], prev_dev(kk),
                    ).wait_recv()

    dots_k = jnp.zeros((TOK, DH), F32)
    for h in range(HALF):
        for sib in (False, True):
            g, _, pk, pv = parts(h, sib)
            up = pk.astype(F32) + rn[1, g].astype(F32) + rp[1, g].astype(F32)
            up = up * kg_ref[pl.ds(g, 1), :]
            gk[g] = up
            dots_k = dots_k + up * kraw[g].astype(F32)
            ov_ref[g] = (pv.astype(F32) + rn[0, g].astype(F32) + rp[0, g].astype(F32)).astype(BF)
    sd_a[...] = jnp.zeros_like(sd_a)
    dot_q, dot_k = all_sum((lanes_sum_row(dots_q), lanes_sum_row(dots_k)), sd_a, sd_b, 1)
    cq = invq[...] * invq[...] * invq[...] * row_to_full(dot_q / features)
    ck = invk[...] * invk[...] * invk[...] * row_to_full(dot_k / features)
    for g in range(LOC):
        oq_ref[g] = (invq[...] * gq[g] - qraw[g].astype(F32) * cq).astype(BF)
        ok_ref[g] = (invk[...] * gk[g] - kraw[g].astype(F32) * ck).astype(BF)

    for c in to_sib:
        c.wait_send()

    @pl.when(has_next)
    def _():
        for arr in range(2):
            for h in range(HALF):
                for kk in range(2):
                    fwd_next(arr, h, kk).wait_send()
                ret_next(arr, h).wait_send()

    @pl.when(has_prev)
    def _():
        for arr in range(2):
            for h in range(HALF):
                for kk in range(2):
                    ret_prev(arr, h, kk).wait_send()

    @pl.when(has_prev & (core == 0))
    def _():
        for arr in range(2):
            for h in range(HALF):
                for kk in range(2):
                    fwd_prev(arr, h, kk).wait_send()

    for arr in range(3):
        for h in range(HALF):
            ret_sib(arr, h).wait_send()


def local(queries, keys, values, out_grads, query_gain, key_gain, block_lengths):
    nctx, nx = lax.axis_size("ctx"), lax.axis_size("head")
    heads_first = [jnp.moveaxis(a, 1, 0) for a in (queries, keys, values, out_grads)]
    big = (LOC, TOK, DH)
    dma = pltpu.SemaphoreType.DMA
    vmem = pltpu.VMEM
    out = jax.ShapeDtypeStruct(big, BF)
    any_spec = pl.BlockSpec(memory_space=pl.ANY)
    vmem_spec = pl.BlockSpec(memory_space=pltpu.VMEM)
    res = pl.pallas_call(
        functools.partial(body, nctx, nx),
        out_shape=(out, out, out),
        in_specs=[any_spec] * 4 + [vmem_spec] * 3,
        out_specs=(vmem_spec, vmem_spec, vmem_spec),
        scratch_shapes=[
            vmem(big, BF), vmem(big, BF), vmem(big, BF), vmem(big, BF),
            vmem((HALF, SPAN, DH), BF), vmem((HALF, SPAN, DH), BF),
            vmem((HALF, PAIR, DH), BF), vmem((HALF, PAIR, DH), BF),
            vmem((TOK, DH), F32), vmem((TOK, DH), F32),
            vmem((8, TOK), F32), vmem((nx - 1, 8, TOK), F32),
            vmem((8, TOK), F32), vmem((nx - 1, 8, TOK), F32),
            vmem((NQ, WIN, QT), F32), vmem((WIN, QT), F32), vmem((WIN, QT), F32),
            vmem((DH, SPAN), BF), vmem((SPAN, DH), F32), vmem((SPAN, DH), F32),
            vmem((HALF, SPAN, DH), BF), vmem((HALF, SPAN, DH), BF), vmem((HALF, PAIR, DH), BF),
            vmem((2,) + big, BF), vmem((2,) + big, BF), vmem((3, HALF, TOK, DH), BF),
            vmem(big, F32), vmem(big, F32),
            dma((6,)),
            dma((2, HALF, 2)), dma((2, HALF, 2)), dma((2, HALF, 2)), dma((2, HALF)),
            dma((4,)), dma((4,)), dma((2, 3)), dma((2, 3)),
            dma((2, HALF, 2)), dma((2, HALF, 2)), dma((2, HALF)), dma((2, HALF, 2)),
            dma((3, HALF)), dma((3, HALF)),
        ],
        compiler_params=pltpu.CompilerParams(
            collective_id=0, has_side_effects=True, vmem_limit_bytes=56 << 20
        ),
    )(*heads_first, query_gain, key_gain, block_lengths.reshape(1, -1))
    return tuple(jnp.moveaxis(a, 0, 1) for a in res)


def solution(mesh):
    placed = (
        P("ctx", "head", None),
        P("ctx", "head", None),
        P("ctx", "head", None),
        P("ctx", "head", None),
        P("head", None),
        P("head", None),
        P(),
    )
    return jax.shard_map(
        local,
        mesh=mesh,
        in_specs=placed,
        out_specs=(P("ctx", "head", None), P("ctx", "head", None), P("ctx", "head", None)),
        check_vma=False,
    )
```

```python
import functools

import jax
import jax.numpy as jnp
from jax import lax
from jax.experimental import pallas as pl
from jax.experimental.pallas import tpu as pltpu
from jax.sharding import PartitionSpec as P

MESH = pl.DeviceIdType.MESH
norm_eps = 1e-06
hidden = -1e30
BF = jnp.bfloat16
F32 = jnp.float32

TOK = 384
PAIR = 2 * TOK
SPAN = 5 * TOK
LOC = 6
HALF = 3
DH = 128
QT = 256
NQ = PAIR // QT
WIN = 1408
KC = 128
NK = WIN // KC


def dot(a, b):
    return jnp.dot(a, b, preferred_element_type=F32)


def lanes_sum_row(x):
    return jnp.sum(x.T, axis=0, keepdims=True)


def row_to_full(row):
    return jnp.broadcast_to(row, (DH, row.shape[1])).T


def body(
    nctx, nx,
    q_hbm, k_hbm, v_hbm, d_hbm, qg_hbm, kg_hbm, len_hbm,
    oq_ref, ok_ref, ov_ref,
    qg_ref, kg_ref, len_ref, qraw, kraw, qn, kn, kw, vw, qw, dw,
    invq, invk, st_a, st_b, sd_a, sd_b,
    bias, sbuf, pbuf, kt, dk_acc, dv_acc, ek, eq, e_snd, e_rcv, i_snd, i_rcv,
    snd, dq_snd, rn, rp, rs, rs_q, gq, gk,
    lsem, s_fn, r_fn, s_fp, r_fp, s_sib, r_sib, s_x, r_x, s_rp, r_rn, s_rn, r_rp, s_rs, r_rs, s_e, r_e, s_i, r_i,
):
    me = lax.axis_index("ctx")
    x = lax.axis_index("head")
    core = lax.rem(me, 2)
    chip = me // 2
    chips = nctx // 2
    has_prev = chip > 0
    has_next = chip < chips - 1
    other = 1 - core
    features = float(nx * LOC * DH)
    scale = DH ** -0.5
    log2e = 1.4426950408889634
    sib_dev = (2 * chip + other, x)
    x_devs = [(me, lax.rem(x + d, nx)) for d in range(1, nx)]

    def next_dev(kk):
        return (2 * chip + 2 + kk, x)

    def prev_dev(kk):
        return (2 * chip - 2 + kk, x)

    def remote(src, dst, ss, rs_, dev):
        return pltpu.make_async_remote_copy(
            src_ref=src, dst_ref=dst, send_sem=ss, recv_sem=rs_, device_id=dev, device_id_type=MESH
        )

    bar = pltpu.get_barrier_semaphore()

    @pl.when(has_next)
    def _():
        for kk in range(2):
            pl.semaphore_signal(bar, inc=1, device_id=next_dev(kk), device_id_type=MESH)

    @pl.when(has_prev)
    def _():
        for kk in range(2):
            pl.semaphore_signal(bar, inc=1, device_id=prev_dev(kk), device_id_type=MESH)

    pl.semaphore_signal(bar, inc=1, device_id=sib_dev, device_id_type=MESH)
    for dev in x_devs:
        pl.semaphore_signal(bar, inc=1, device_id=dev, device_id_type=MESH)

    own = pl.ds(pl.multiple_of(core * TOK, TOK), TOK)
    own_win = pl.ds(pl.multiple_of(PAIR + core * TOK, TOK), TOK)
    own_heads = pl.ds(core * HALF, HALF)
    sib_heads = pl.ds(other * HALF, HALF)
    load_k = pltpu.make_async_copy(k_hbm, kraw, lsem.at[0])
    load_q = pltpu.make_async_copy(q_hbm, qraw, lsem.at[1])
    self_v = pltpu.make_async_copy(v_hbm.at[own_heads], vw.at[:, own_win], lsem.at[2])
    self_d = pltpu.make_async_copy(d_hbm.at[own_heads], dw.at[:, own], lsem.at[3])
    load_small = [
        pltpu.make_async_copy(qg_hbm, qg_ref, lsem.at[6]),
        pltpu.make_async_copy(kg_hbm, kg_ref, lsem.at[7]),
        pltpu.make_async_copy(len_hbm, len_ref, lsem.at[8]),
    ]
    load_k.start()
    load_q.start()
    self_v.start()
    self_d.start()
    for c in load_small:
        c.start()

    @pl.when(has_prev & has_next)
    def _():
        pl.semaphore_wait(bar, nx + 4)

    @pl.when(jnp.logical_not(has_prev & has_next))
    def _():
        pl.semaphore_wait(bar, nx + 2)

    def fwd_next(arr, h, kk):
        src = (v_hbm, kn if h else k_hbm)[arr].at[kk * HALF + h]
        dst = (vw, kw)[arr].at[h, own]
        return remote(src, dst, s_fn.at[arr, h, kk], r_fn.at[arr, h, core], next_dev(kk))

    def fwd_prev(arr, h, kk):
        src = (v_hbm, kn if h else k_hbm)[arr].at[kk * HALF + h]
        dst = (vw, kw)[arr].at[h, pl.ds(2 * PAIR, TOK)]
        return remote(src, dst, s_fp.at[arr, h, kk], r_fp.at[arr, h], prev_dev(kk))

    def go_next(arr, h):
        @pl.when(has_next)
        def _():
            for kk in range(2):
                fwd_next(arr, h, kk).start()

    def go_prev(arr, h):
        @pl.when(has_prev & (core == 0))
        def _():
            for kk in range(2):
                fwd_prev(arr, h, kk).start()

    to_sib = [
        remote(v_hbm.at[sib_heads], vw.at[:, own_win], s_sib.at[0], r_sib.at[0], sib_dev),
        remote(d_hbm.at[sib_heads], dw.at[:, own], s_sib.at[1], r_sib.at[1], sib_dev),
        remote(kn.at[sib_heads], kw.at[:, own_win], s_sib.at[2], r_sib.at[2], sib_dev),
        remote(qn.at[sib_heads], qw.at[:, own], s_sib.at[3], r_sib.at[3], sib_dev),
    ]
    go_next(0, 0)
    go_prev(0, 0)
    go_next(1, 0)
    go_prev(1, 0)
    go_prev(0, 1)
    to_sib[0].start()
    to_sib[1].start()

    def sum_start(rows, mine, theirs, rnd):
        mine[0:1, :] = rows[0]
        mine[1:2, :] = rows[1]
        copies = [
            remote(mine, theirs.at[d], s_x.at[rnd, d], r_x.at[rnd, d], x_devs[d]) for d in range(nx - 1)
        ]
        for c in copies:
            c.start()
        return copies

    def sum_done(copies, mine, theirs):
        for c in copies:
            c.wait()
        total = mine[0:2, :]
        for d in range(nx - 1):
            total = total + theirs[d, 0:2, :]
        return total[0:1, :], total[1:2, :]

    def inv_next(kk):
        return remote(i_snd, i_rcv.at[core], s_i.at[kk], r_i.at[core], next_dev(kk))

    def inv_prev(kk):
        return remote(i_snd, i_rcv.at[2], s_i.at[2 + kk], r_i.at[2], prev_dev(kk))

    def squares(ref):
        total = jnp.zeros((TOK, DH), F32)
        for g in range(LOC):
            v = ref[g].astype(F32)
            total = total + v * v
        return lanes_sum_row(total)

    load_q.wait()
    load_k.wait()
    for c in load_small:
        c.wait()
    for small in (st_a, sd_a, e_snd, e_rcv, i_snd):
        small[...] = jnp.zeros_like(small)
    squares_x = sum_start((squares(qraw), squares(kraw)), st_a, st_b, 0)
    sum_q, sum_k = sum_done(squares_x, st_a, st_b)
    row_invk = lax.rsqrt(sum_k / features + norm_eps)
    i_snd[0:1] = row_invk

    @pl.when(has_next)
    def _():
        for kk in range(2):
            inv_next(kk).start()

    @pl.when(has_prev & (core == 0))
    def _():
        for kk in range(2):
            inv_prev(kk).start()

    invk[...] = row_to_full(row_invk)
    invq[...] = row_to_full(lax.rsqrt(sum_q / features + norm_eps))
    for h in (1, 2, 0):
        for kk in range(2):
            g = kk * HALF + h
            kn[g] = (kraw[g].astype(F32) * invk[...] * kg_ref[g : g + 1, :]).astype(BF)
        if h:
            go_next(1, h)
            go_next(0, h)
            go_prev(1, h)
            if h == 2:
                go_prev(0, 2)
    to_sib[2].start()
    for g in range(LOC):
        qn[g] = (qraw[g].astype(F32) * invq[...] * qg_ref[g : g + 1, :]).astype(BF)
    to_sib[3].start()
    self_k = pltpu.make_async_copy(kn.at[own_heads], kw.at[:, own_win], lsem.at[4])
    self_q = pltpu.make_async_copy(qn.at[own_heads], qw.at[:, own], lsem.at[5])
    self_k.start()
    self_q.start()

    @pl.when(jnp.logical_not(has_prev))
    def _():
        for h in range(HALF):
            kw[h, 0:PAIR] = jnp.zeros((PAIR, DH), BF)
            vw[h, 0:PAIR] = jnp.zeros((PAIR, DH), BF)

    @pl.when(jnp.logical_not(has_next))
    def _():
        for h in range(HALF):
            kw[h, 2 * PAIR : SPAN] = jnp.zeros((TOK, DH), BF)
            vw[h, 2 * PAIR : SPAN] = jnp.zeros((TOK, DH), BF)
        rn[...] = jnp.zeros_like(rn)

    @pl.when(jnp.logical_not(has_prev & (core == 0)))
    def _():
        rp[...] = jnp.zeros_like(rp)

    nb = len_ref.shape[1]
    lens = len_ref[...].astype(F32)
    ri = lax.broadcasted_iota(jnp.int32, (nb, nb), 0)
    ci = lax.broadcasted_iota(jnp.int32, (nb, nb), 1)
    ends_col = jnp.sum(jnp.where(ci <= ri, lens, 0.0), axis=1, keepdims=True)
    start = chip * PAIR - PAIR
    pos = (start + lax.broadcasted_iota(jnp.int32, (1, SPAN), 1)).astype(F32)
    blocks = jnp.sum(jnp.where(ends_col <= pos, 1.0, 0.0), axis=0, keepdims=True)
    q_block = blocks[:, PAIR : 2 * PAIR]
    k_block = jnp.where(pos >= 0.0, blocks, -10.0)
    k_full = row_to_full(k_block)
    for t in range(NQ):
        kb = k_full[t * QT : t * QT + WIN]
        for c in range(QT // DH):
            qb = q_block[:, t * QT + c * DH : t * QT + (c + 1) * DH]
            seen = (kb <= qb) & (kb >= qb - 1.0)
            bias[t, :, c * DH : (c + 1) * DH] = jnp.where(seen, 0.0, hidden)

    self_v.wait()
    self_d.wait()
    self_k.wait()
    self_q.wait()
    for c in to_sib:
        c.wait_recv()

    pieces = ((0, 256, 0, 0), (256, 128, 0, 256), (384, 128, 1, 0), (512, 256, 1, 128))

    def ret_prev(h, i):
        row, rows, kk, to = pieces[i]
        src = snd.at[h, :, pl.ds(row, rows)]
        dst = rn.at[:, core * HALF + h, pl.ds(to, rows)]
        return remote(src, dst, s_rp.at[h, i], r_rn.at[h, core, i % 2], prev_dev(kk))

    def ret_next(h):
        src = snd.at[h, :, pl.ds(2 * PAIR, TOK)]
        dst = rp.at[:, core * HALF + h]
        return remote(src, dst, s_rn.at[h], r_rp.at[h, core], next_dev(0))

    def ret_sib(h):
        rows = pl.ds(pl.multiple_of(PAIR + other * TOK, TOK), TOK)
        return remote(snd.at[h, :, rows], rs.at[h], s_rs.at[0, h], r_rs.at[0, h], sib_dev)

    def ret_sib_q(h):
        rows = pl.ds(pl.multiple_of(other * TOK, TOK), TOK)
        return remote(dq_snd.at[h, rows], rs_q.at[h], s_rs.at[1, h], r_rs.at[1, h], sib_dev)

    def dots_prev(kk):
        return remote(e_snd.at[kk], e_rcv.at[1 + core], s_e.at[kk], r_e.at[1 + core], prev_dev(kk))

    def dots_sib():
        return remote(e_snd.at[2 + other], e_rcv.at[0], s_e.at[2], r_e.at[0], sib_dev)

    def dots_next():
        return remote(e_snd.at[4], e_rcv.at[3 + core], s_e.at[3], r_e.at[3 + core], next_dev(0))

    def pack(h, row, rows):
        snd[h, 0, row : row + rows] = dv_acc[row : row + rows].astype(BF)
        snd[h, 1, row : row + rows] = (dk_acc[row : row + rows] * scale).astype(BF)

    def add_dots(h, row, rows):
        at = slice(row, row + rows)
        ek[at] = ek[at] + dk_acc[at] * kw[h, at].astype(F32)

    def leave(h, t):
        @pl.when(t == 0)
        def _():
            pack(h, 0, 256)

            @pl.when(has_prev)
            def _():
                ret_prev(h, 0).start()

            add_dots(h, 0, 256)

        @pl.when(t == 1)
        def _():
            pack(h, 256, 256)

            @pl.when(has_prev)
            def _():
                ret_prev(h, 1).start()
                ret_prev(h, 2).start()

            add_dots(h, 256, 256)

        @pl.when(t == 2)
        def _():
            add_dots(h, 512, SPAN - 512)

            @pl.when(h == HALF - 1)
            def _():
                row = lanes_sum_row(ek[...]) * scale
                row_q = lanes_sum_row(eq[...])
                e_snd[0, 0:1] = row[:, 0:TOK]
                e_snd[1, 0:1] = row[:, TOK : 2 * TOK]
                for c in range(2):
                    e_snd[2 + c, 0:1] = row_q[:, c * TOK : (c + 1) * TOK]
                    e_snd[2 + c, 1:2] = row[:, PAIR + c * TOK : PAIR + (c + 1) * TOK]
                e_snd[4, 0:1] = row[:, 2 * PAIR : SPAN]

                @pl.when(has_prev)
                def _():
                    for kk in range(2):
                        dots_prev(kk).start()

                @pl.when(has_next)
                def _():
                    dots_next().start()

                dots_sib().start()

            pack(h, 512, SPAN - 512)

            @pl.when(has_prev)
            def _():
                ret_prev(h, 3).start()

            @pl.when(has_next)
            def _():
                ret_next(h).start()

            ret_sib(h).start()
            ret_sib_q(h).start()

    def inv_next_done(kk):
        return remote(i_snd, i_rcv.at[kk], s_i.at[kk], r_i.at[kk], prev_dev(kk))

    def inv_prev_done():
        return remote(i_snd, i_rcv.at[2], s_i.at[2], r_i.at[2], next_dev(0))

    def tile(h, t):
        first = pl.multiple_of(t * QT, QT)
        q_rows = qw[h, pl.ds(first, QT)]
        d_rows = dw[h, pl.ds(first, QT)]
        q_t = q_rows.T
        d_t = d_rows.T

        def keys_at(j):
            return pl.ds(pl.multiple_of(first + j * KC, KC), KC)

        top = jnp.full((8, QT), -3e38, F32)
        for j in range(NK):
            s = dot(kw[h, keys_at(j)], q_t) + bias[t, j * KC : (j + 1) * KC]
            sbuf[j * KC : (j + 1) * KC] = s
            top = jnp.maximum(top, jnp.max(s.reshape(KC // 8, 8, QT), axis=0))
        top = jnp.max(top, axis=0, keepdims=True)
        total = jnp.zeros((8, QT), F32)
        delta = jnp.zeros((8, QT), F32)
        for j in range(NK):
            rows = slice(j * KC, (j + 1) * KC)
            p = jnp.exp2((sbuf[rows] - top) * (scale * log2e))
            dp = dot(vw[h, keys_at(j)], d_t)
            pbuf[rows] = p
            sbuf[rows] = dp
            total = total + jnp.sum(p.reshape(KC // 8, 8, QT), axis=0)
            delta = delta + jnp.sum((p * dp).reshape(KC // 8, 8, QT), axis=0)
        inverse = 1.0 / jnp.sum(total, axis=0, keepdims=True)
        delta = jnp.sum(delta, axis=0, keepdims=True) * inverse
        inv_full = row_to_full(inverse)
        q_r = (q_rows.astype(F32) * inv_full).astype(BF)
        d_r = (d_rows.astype(F32) * inv_full).astype(BF)
        dq_t = jnp.zeros((DH, QT), F32)
        for j in range(NK):
            rows = slice(j * KC, (j + 1) * KC)
            p = pbuf[rows]
            ds = (p * (sbuf[rows] - delta)).astype(BF)
            at = keys_at(j)
            dv_acc[at] = dv_acc[at] + dot(p.astype(BF), d_r)
            dk_acc[at] = dk_acc[at] + dot(ds, q_r)
            dq_t = dq_t + dot(kt[:, at], ds)
        dq = (dq_t * (inverse * scale)).T
        dq_snd[h, pl.ds(first, QT)] = dq.astype(BF)
        eq[pl.ds(first, QT)] = eq[pl.ds(first, QT)] + dq * q_rows.astype(F32)
        leave(h, t)

    def head(h, carry):
        @pl.when(has_prev)
        def _():
            for arr in range(2):
                for kk in range(2):
                    remote(
                        v_hbm.at[0], (vw, kw)[arr].at[h, pl.ds(kk * TOK, TOK)],
                        s_fn.at[arr, h, kk], r_fn.at[arr, h, kk], prev_dev(kk),
                    ).wait_recv()

        @pl.when(has_next)
        def _():
            for arr in range(2):
                remote(
                    v_hbm.at[0], (vw, kw)[arr].at[h, pl.ds(2 * PAIR, TOK)],
                    s_fp.at[arr, h, 0], r_fp.at[arr, h], next_dev(0),
                ).wait_recv()

        @pl.when(h == 0)
        def _():
            gain = kg_ref[pl.ds(core * HALF, 1), :]

            def normed(slot, row):
                at = slice(row, row + TOK)
                full = row_to_full(i_rcv[slot, 0:1])
                kw[0, at] = (kw[0, at].astype(F32) * full * gain).astype(BF)

            @pl.when(has_prev)
            def _():
                for kk in range(2):
                    inv_next_done(kk).wait_recv()
                    normed(kk, kk * TOK)

            @pl.when(has_next)
            def _():
                inv_prev_done().wait_recv()
                normed(2, 2 * PAIR)

        for j in range(SPAN // KC):
            kt[:, j * KC : (j + 1) * KC] = kw[h, j * KC : (j + 1) * KC].T
        dk_acc[...] = jnp.zeros_like(dk_acc)
        dv_acc[...] = jnp.zeros_like(dv_acc)
        lax.fori_loop(0, NQ, lambda t, c: (tile(h, t), c)[1], 0)
        return carry

    ek[...] = jnp.zeros_like(ek)
    eq[...] = jnp.zeros_like(eq)
    lax.fori_loop(0, HALF, head, 0)

    for h in range(HALF):
        ret_sib(h).wait_recv()
        ret_sib_q(h).wait_recv()

    def from_next(h):
        @pl.when(has_next)
        def _():
            for kk in range(2):
                for c in range(2):
                    @pl.when(core == c)
                    def _():
                        for i in range(2):
                            _, rows, _, to = pieces[2 * c + i]
                            at = rn.at[:, kk * HALF + h, pl.ds(to, rows)]
                            remote(at, at, s_rp.at[h, 2 * c + i], r_rn.at[h, kk, i], next_dev(kk)).wait_recv()

    def from_prev(h):
        @pl.when(has_prev & (core == 0))
        def _():
            for kk in range(2):
                at = rp.at[:, kk * HALF + h]
                remote(at, at, s_rn.at[h], r_rp.at[h, kk], prev_dev(kk)).wait_recv()

    def own_grads(h, sib):
        g = (other if sib else core) * HALF + h
        if sib:
            return g, rs[h, 0], rs[h, 1]
        return g, snd[h, 0, own_win], snd[h, 1, own_win]

    def gather_kv(h):
        for sib in (False, True):
            g, pv, pk = own_grads(h, sib)
            up = pk.astype(F32) + rn[1, g].astype(F32) + rp[1, g].astype(F32)
            gk[g] = up * kg_ref[pl.ds(g, 1), :]
            ov_ref[g] = (pv.astype(F32) + rn[0, g].astype(F32) + rp[0, g].astype(F32)).astype(BF)

    for h in range(HALF):
        for sib in (False, True):
            g = (other if sib else core) * HALF + h
            pq = rs_q[h] if sib else dq_snd[h, own]
            gq[g] = pq.astype(F32) * qg_ref[pl.ds(g, 1), :]

    for h in range(HALF - 1):
        from_next(h)
        from_prev(h)
        gather_kv(h)

    dots_sib().wait_recv()

    @pl.when(has_next)
    def _():
        for kk in range(2):
            at = e_rcv.at[1 + kk]
            remote(at, at, s_e.at[kk], r_e.at[1 + kk], next_dev(kk)).wait_recv()

    @pl.when(has_prev & (core == 0))
    def _():
        for kk in range(2):
            at = e_rcv.at[3 + kk]
            remote(at, at, s_e.at[3], r_e.at[3 + kk], prev_dev(kk)).wait_recv()

    both = e_snd[2 + core] + e_rcv[0]
    row_k = both[1:2] + (e_rcv[1, 0:1] + e_rcv[2, 0:1]) + (e_rcv[3, 0:1] + e_rcv[4, 0:1])
    dots_x = sum_start((both[0:1], row_k), sd_a, sd_b, 1)
    dot_q, dot_k = sum_done(dots_x, sd_a, sd_b)
    cq = invq[...] * invq[...] * row_to_full(dot_q / features)
    ck = invk[...] * invk[...] * row_to_full(dot_k / features)
    for g in range(LOC):
        oq_ref[g] = (invq[...] * gq[g] - qraw[g].astype(F32) * cq).astype(BF)

    def finish_k(h):
        for sib in (False, True):
            g = (other if sib else core) * HALF + h
            ok_ref[g] = (invk[...] * gk[g] - kraw[g].astype(F32) * ck).astype(BF)

    for h in range(HALF - 1):
        finish_k(h)
    from_next(HALF - 1)
    from_prev(HALF - 1)
    gather_kv(HALF - 1)
    finish_k(HALF - 1)

    for c in to_sib:
        c.wait_send()

    @pl.when(has_next)
    def _():
        for arr in range(2):
            for h in range(HALF):
                for kk in range(2):
                    fwd_next(arr, h, kk).wait_send()
        for h in range(HALF):
            ret_next(h).wait_send()
        dots_next().wait_send()
        for kk in range(2):
            inv_next(kk).wait_send()

    @pl.when(has_prev)
    def _():
        for h in range(HALF):
            for i in range(4):
                ret_prev(h, i).wait_send()
        for kk in range(2):
            dots_prev(kk).wait_send()

    @pl.when(has_prev & (core == 0))
    def _():
        for arr in range(2):
            for h in range(HALF):
                for kk in range(2):
                    fwd_prev(arr, h, kk).wait_send()
        for kk in range(2):
            inv_prev(kk).wait_send()

    for h in range(HALF):
        ret_sib(h).wait_send()
        ret_sib_q(h).wait_send()
    dots_sib().wait_send()


def local(queries, keys, values, out_grads, query_gain, key_gain, block_lengths):
    nctx, nx = lax.axis_size("ctx"), lax.axis_size("head")
    heads_first = [jnp.moveaxis(a, 1, 0) for a in (queries, keys, values, out_grads)]
    big = (LOC, TOK, DH)
    dma = pltpu.SemaphoreType.DMA
    vmem = pltpu.VMEM
    out = jax.ShapeDtypeStruct(big, BF)
    any_spec = pl.BlockSpec(memory_space=pl.ANY)
    vmem_spec = pl.BlockSpec(memory_space=pltpu.VMEM)
    res = pl.pallas_call(
        functools.partial(body, nctx, nx),
        out_shape=(out, out, out),
        in_specs=[pl.BlockSpec(memory_space=pltpu.HBM)] * 7,
        out_specs=(vmem_spec, vmem_spec, vmem_spec),
        scratch_shapes=[
            vmem((LOC, DH), F32), vmem((LOC, DH), F32), vmem((1, block_lengths.shape[0]), jnp.int32),
            vmem(big, BF), vmem(big, BF), vmem(big, BF), vmem(big, BF),
            vmem((HALF, SPAN, DH), BF), vmem((HALF, SPAN, DH), BF),
            vmem((HALF, PAIR, DH), BF), vmem((HALF, PAIR, DH), BF),
            vmem((TOK, DH), F32), vmem((TOK, DH), F32),
            vmem((8, TOK), F32), vmem((nx - 1, 8, TOK), F32),
            vmem((8, TOK), F32), vmem((nx - 1, 8, TOK), F32),
            vmem((NQ, WIN, QT), F32), vmem((WIN, QT), F32), vmem((WIN, QT), F32),
            vmem((DH, SPAN), BF), vmem((SPAN, DH), F32), vmem((SPAN, DH), F32),
            vmem((SPAN, DH), F32), vmem((PAIR, DH), F32), vmem((5, 8, TOK), F32), vmem((5, 8, TOK), F32),
            vmem((8, TOK), F32), vmem((3, 8, TOK), F32),
            vmem((HALF, 2, SPAN, DH), BF), vmem((HALF, PAIR, DH), BF),
            vmem((2,) + big, BF), vmem((2,) + big, BF), vmem((HALF, 2, TOK, DH), BF), vmem((HALF, TOK, DH), BF),
            vmem(big, F32), vmem(big, F32),
            dma((9,)),
            dma((2, HALF, 2)), dma((2, HALF, 2)), dma((2, HALF, 2)), dma((2, HALF)),
            dma((4,)), dma((4,)), dma((2, 3)), dma((2, 3)),
            dma((HALF, 4)), dma((HALF, 2, 2)), dma((HALF,)), dma((HALF, 2)),
            dma((2, HALF)), dma((2, HALF)), dma((4,)), dma((5,)), dma((4,)), dma((3,)),
        ],
        compiler_params=pltpu.CompilerParams(
            collective_id=0, has_side_effects=True, vmem_limit_bytes=52 << 20
        ),
    )(*heads_first, query_gain, key_gain, block_lengths.reshape(1, -1))
    return tuple(jnp.moveaxis(a, 0, 1) for a in res)


def solution(mesh):
    placed = (
        P("ctx", "head", None),
        P("ctx", "head", None),
        P("ctx", "head", None),
        P("ctx", "head", None),
        P("head", None),
        P("head", None),
        P(),
    )
    return jax.shard_map(
        local,
        mesh=mesh,
        in_specs=placed,
        out_specs=(P("ctx", "head", None), P("ctx", "head", None), P("ctx", "head", None)),
        check_vma=False,
    )
```

```python
import functools

import jax
import jax.numpy as jnp
from jax import lax
from jax.experimental import pallas as pl
from jax.experimental.pallas import tpu as pltpu
from jax.sharding import PartitionSpec as P

MESH = pl.DeviceIdType.MESH
norm_eps = 1e-06
hidden = -1e30
BF = jnp.bfloat16
F32 = jnp.float32

TOK = 384
PAIR = 2 * TOK
CUT = TOK // 2
BACK = 640
OWN_END = BACK + PAIR
SPAN = OWN_END + TOK
LOC = 6
HALF = 3
DH = 128
QT = 256
NQ = PAIR // QT + 1
ROWS_Q = NQ * QT
WIN = 1408
KC = 128
NK = WIN // KC
tile_first = (0, 128, 384, 640)
tile_steps = (NK - 1, NK, NK, 8)


def dot(a, b):
    return jnp.dot(a, b, preferred_element_type=F32)


def lanes_sum_row(x):
    return jnp.sum(x.T, axis=0, keepdims=True)


def row_to_full(row):
    return jnp.broadcast_to(row, (DH, row.shape[1])).T


def body(
    nctx, nx,
    q_hbm, k_hbm, v_hbm, d_hbm, qg_hbm, kg_hbm, len_hbm,
    oq_ref, ok_ref, ov_ref,
    qg_ref, kg_ref, len_ref, qraw, kraw, vhalf, dhalf, qn, kn, kw, vw, qw, dw, two_snd, two_rcv,
    invq, invk, st_a, st_b,
    bias, active, sbuf, pbuf, kt, dk_acc, dv_acc, ek, eq, e_snd, e_x, e_sum, e_rcv, i_snd, i_rcv,
    snd, dq_snd, up_snd, rn, rp, rp2, rs, rs_q, gq, gk,
    lsem, s_fn, r_fn, s_fp, r_fp, s_sib, r_sib, s_x, r_x, s_rp, r_rn, s_rn, r_rp, s_rs, r_rs, s_e, r_e, s_i, r_i, s_two, r_two, s_up, r_up,
):
    me = lax.axis_index("ctx")
    x = lax.axis_index("head")
    core = lax.rem(me, 2)
    chip = me // 2
    chips = nctx // 2
    has_prev = chip > 0
    has_next = chip < chips - 1
    other = 1 - core
    features = float(nx * LOC * DH)
    scale = DH ** -0.5
    log2e = 1.4426950408889634
    sib_dev = (2 * chip + other, x)
    x_devs = [(me, lax.rem(x + d, nx)) for d in range(1, nx)]

    def next_dev(kk):
        return (2 * chip + 2 + kk, x)

    def prev_dev(kk):
        return (2 * chip - 2 + kk, x)

    def remote(src, dst, ss, rs_, dev):
        return pltpu.make_async_remote_copy(
            src_ref=src, dst_ref=dst, send_sem=ss, recv_sem=rs_, device_id=dev, device_id_type=MESH
        )

    bar = pltpu.get_barrier_semaphore()

    @pl.when(has_next)
    def _():
        for kk in range(2):
            pl.semaphore_signal(bar, inc=1, device_id=next_dev(kk), device_id_type=MESH)

    @pl.when(has_prev)
    def _():
        for kk in range(2):
            pl.semaphore_signal(bar, inc=1, device_id=prev_dev(kk), device_id_type=MESH)

    pl.semaphore_signal(bar, inc=1, device_id=sib_dev, device_id_type=MESH)
    for dev in x_devs:
        pl.semaphore_signal(bar, inc=1, device_id=dev, device_id_type=MESH)

    own = pl.ds(pl.multiple_of(core * TOK, TOK), TOK)
    own_win = pl.ds(pl.multiple_of(BACK + core * TOK, 128), TOK)
    own_heads = pl.ds(core * HALF, HALF)
    sib_heads = pl.ds(other * HALF, HALF)
    load_k = pltpu.make_async_copy(k_hbm, kraw, lsem.at[0])
    load_q = pltpu.make_async_copy(q_hbm, qraw, lsem.at[1])
    self_v = pltpu.make_async_copy(v_hbm.at[own_heads], vw.at[:, own_win], lsem.at[2])
    self_d = pltpu.make_async_copy(d_hbm.at[own_heads], dw.at[:, own], lsem.at[3])
    load_small = [
        pltpu.make_async_copy(qg_hbm, qg_ref, lsem.at[6]),
        pltpu.make_async_copy(kg_hbm, kg_ref, lsem.at[7]),
        pltpu.make_async_copy(len_hbm, len_ref, lsem.at[8]),
    ]
    load_vh = pltpu.make_async_copy(v_hbm.at[:, pl.ds(CUT, CUT)], vhalf, lsem.at[9])
    load_dh = pltpu.make_async_copy(d_hbm.at[:, pl.ds(0, CUT)], dhalf, lsem.at[10])
    load_k.start()
    load_q.start()
    self_v.start()
    self_d.start()
    for c in load_small:
        c.start()
    load_vh.start()
    load_dh.start()

    @pl.when(has_prev & has_next)
    def _():
        pl.semaphore_wait(bar, nx + 4)

    @pl.when(jnp.logical_not(has_prev & has_next))
    def _():
        pl.semaphore_wait(bar, nx + 2)

    def fwd_next(arr, h, kk, c):
        src = (v_hbm, kn if h else k_hbm)[arr].at[kk * HALF + h]
        if c == 0:
            src = src.at[pl.ds(CUT, CUT)]
            dst = (vw, kw)[arr].at[h, pl.ds(BACK - TOK - CUT, CUT)]
        else:
            dst = (vw, kw)[arr].at[h, pl.ds(BACK - TOK, TOK)]
        return remote(src, dst, s_fn.at[arr, h, kk], r_fn.at[arr, h, c], next_dev(kk))

    def fwd_prev(arr, h, kk):
        src = (v_hbm, kn if h else k_hbm)[arr].at[kk * HALF + h, pl.ds(0, CUT)]
        dst = (vw, kw)[arr].at[h, pl.ds(OWN_END, CUT)]
        return remote(src, dst, s_fp.at[arr, h, kk], r_fp.at[arr, h], prev_dev(kk))

    def two_prev(arr, h, kk):
        return remote(
            two_snd.at[kk * HALF + h, arr], two_rcv.at[h, arr], s_two.at[arr, h, kk], r_two.at[arr, h], prev_dev(kk)
        )

    def at_core(c, cond):
        return cond & (core == c)

    def go_next(arr, h):
        for c in range(2):
            @pl.when(at_core(c, has_next))
            def _():
                for kk in range(2):
                    fwd_next(arr, h, kk, c).start()

    def go_prev(arr, h):
        @pl.when(at_core(0, has_prev))
        def _():
            for kk in range(2):
                fwd_prev(arr, h, kk).start()

    def go_two(arr):
        @pl.when(at_core(0, has_prev))
        def _():
            for h in range(HALF):
                for kk in range(2):
                    two_prev(arr, h, kk).start()

    to_sib = [
        remote(v_hbm.at[sib_heads], vw.at[:, own_win], s_sib.at[0], r_sib.at[0], sib_dev),
        remote(d_hbm.at[sib_heads], dw.at[:, own], s_sib.at[1], r_sib.at[1], sib_dev),
        remote(kn.at[sib_heads], kw.at[:, own_win], s_sib.at[2], r_sib.at[2], sib_dev),
        remote(qn.at[sib_heads], qw.at[:, own], s_sib.at[3], r_sib.at[3], sib_dev),
    ]
    go_next(0, 0)
    go_prev(0, 0)
    go_next(1, 0)
    go_prev(1, 0)
    go_next(0, 1)
    go_prev(0, 1)
    go_prev(0, 2)
    to_sib[0].start()
    to_sib[1].start()

    def sum_start(rows, mine, theirs, rnd):
        mine[0:1, :] = rows[0]
        mine[1:2, :] = rows[1]
        copies = [
            remote(mine, theirs.at[d], s_x.at[rnd, d], r_x.at[rnd, d], x_devs[d]) for d in range(nx - 1)
        ]
        for c in copies:
            c.start()
        return copies

    def sum_done(copies, mine, theirs):
        for c in copies:
            c.wait()
        total = mine[0:2, :]
        for d in range(nx - 1):
            total = total + theirs[d, 0:2, :]
        return total[0:1, :], total[1:2, :]

    def inv_next(kk):
        return remote(i_snd, i_rcv.at[core], s_i.at[kk], r_i.at[core], next_dev(kk))

    def inv_prev(kk):
        return remote(i_snd, i_rcv.at[2], s_i.at[2 + kk], r_i.at[2], prev_dev(kk))

    def squares(ref):
        total = jnp.zeros((TOK, DH), F32)
        for g in range(LOC):
            v = ref[g].astype(F32)
            total = total + v * v
        return lanes_sum_row(total)

    for c in load_small:
        c.wait()
    nb = len_ref.shape[1]
    lens = len_ref[...].astype(F32)
    ri = lax.broadcasted_iota(jnp.int32, (nb, nb), 0)
    ci = lax.broadcasted_iota(jnp.int32, (nb, nb), 1)
    ends_col = jnp.sum(jnp.where(ci <= ri, lens, 0.0), axis=1, keepdims=True)
    left = (chip * PAIR).astype(F32)
    right = left + PAIR

    def block_end(edge):
        after = jnp.where(ends_col >= edge, ends_col, 1e9) + jnp.zeros((1, DH), F32)
        return jnp.min(after, axis=0, keepdims=True)

    end_left = jnp.where(chip > 0, block_end(left), 0.0)
    end_right = block_end(right)
    early_left = end_left - left <= CUT
    early_right = end_right - right <= CUT
    load_vh.wait()
    load_dh.wait()
    for g in range(LOC):
        two_snd[g, 1] = jnp.where(early_left, dhalf[g], vhalf[g])
    go_two(1)
    load_q.wait()
    load_k.wait()
    for small in (st_a, e_snd, e_rcv, i_snd):
        small[...] = jnp.zeros_like(small)
    squares_x = sum_start((squares(qraw), squares(kraw)), st_a, st_b, 0)
    sum_q, sum_k = sum_done(squares_x, st_a, st_b)
    row_invk = lax.rsqrt(sum_k / features + norm_eps)
    i_snd[0:1] = row_invk

    @pl.when(has_next)
    def _():
        for kk in range(2):
            inv_next(kk).start()

    @pl.when(has_prev & (core == 0))
    def _():
        for kk in range(2):
            inv_prev(kk).start()

    invk[...] = row_to_full(row_invk)
    invq[...] = row_to_full(lax.rsqrt(sum_q / features + norm_eps))
    for h in (1, 2, 0):
        for kk in range(2):
            g = kk * HALF + h
            kn[g] = (kraw[g].astype(F32) * invk[...] * kg_ref[g : g + 1, :]).astype(BF)
        if h:
            go_next(1, h)
            if h > 1:
                go_next(0, h)
            go_prev(1, h)
    to_sib[2].start()
    for g in range(LOC):
        qn[g] = (qraw[g].astype(F32) * invq[...] * qg_ref[g : g + 1, :]).astype(BF)
    for g in range(LOC):
        two_snd[g, 0] = jnp.where(early_left, qn[g, 0:CUT], kn[g, CUT:TOK])
    go_two(0)
    to_sib[3].start()
    self_k = pltpu.make_async_copy(kn.at[own_heads], kw.at[:, own_win], lsem.at[4])
    self_q = pltpu.make_async_copy(qn.at[own_heads], qw.at[:, own], lsem.at[5])
    self_k.start()
    self_q.start()

    for h in range(HALF):
        kw[h, 0 : BACK - TOK - CUT] = jnp.zeros((BACK - TOK - CUT, DH), BF)
        vw[h, 0 : BACK - TOK - CUT] = jnp.zeros((BACK - TOK - CUT, DH), BF)
        qw[h, PAIR + CUT : ROWS_Q] = jnp.zeros((ROWS_Q - PAIR - CUT, DH), BF)
        dw[h, PAIR + CUT : ROWS_Q] = jnp.zeros((ROWS_Q - PAIR - CUT, DH), BF)

    @pl.when(jnp.logical_not(has_prev))
    def _():
        for h in range(HALF):
            kw[h, BACK - TOK - CUT : BACK] = jnp.zeros((TOK + CUT, DH), BF)
            vw[h, BACK - TOK - CUT : BACK] = jnp.zeros((TOK + CUT, DH), BF)

    @pl.when(jnp.logical_not(has_next))
    def _():
        for h in range(HALF):
            kw[h, OWN_END : OWN_END + CUT] = jnp.zeros((CUT, DH), BF)
            vw[h, OWN_END : OWN_END + CUT] = jnp.zeros((CUT, DH), BF)
        two_rcv[...] = jnp.zeros_like(two_rcv)
        rn[...] = jnp.zeros_like(rn)

    @pl.when(at_core(0, has_next))
    def _():
        rn[:, :, 0:CUT] = jnp.zeros((2, LOC, CUT, DH), BF)

    @pl.when(jnp.logical_not(at_core(0, has_prev)))
    def _():
        rp[...] = jnp.zeros_like(rp)
        rp2[...] = jnp.zeros_like(rp2)

    first_pos = chip * PAIR - BACK
    pos = (first_pos + lax.broadcasted_iota(jnp.int32, (1, SPAN), 1)).astype(F32)
    blocks = jnp.sum(jnp.where(ends_col <= pos, 1.0, 0.0), axis=0, keepdims=True)
    q_pos = pos[:, BACK : BACK + ROWS_Q]
    q_block = blocks[:, BACK : BACK + ROWS_Q]
    k_block = jnp.where(pos >= 0.0, blocks, -10.0)
    k_full = row_to_full(k_block)
    for t in range(NQ):
        at, rows = tile_first[t], tile_steps[t] * KC
        kb = k_full[at : at + rows]
        for c in range(QT // DH):
            lanes = slice(c * DH, (c + 1) * DH)
            here = slice(t * QT + c * DH, t * QT + (c + 1) * DH)
            qb = q_block[:, here]
            seen = (kb <= qb) & (kb >= qb - 1.0)
            bias[t, 0:rows, lanes] = jnp.where(seen, 0.0, hidden)
            if t < NQ - 1:
                away = jnp.where(early_left, end_left, 0.0)
                computed = jnp.where(q_pos[:, here] >= away, 1.0, 0.0)
            else:
                until = jnp.where(early_right, end_right, 0.0)
                computed = jnp.where(q_pos[:, here] < until, 1.0, 0.0)
            active[t, 0:1, lanes] = computed

    self_v.wait()
    self_d.wait()
    self_k.wait()
    self_q.wait()
    for c in to_sib:
        c.wait_recv()

    pieces = ((64, 192, 0, 192), (256, 128, 1, 0), (384, 256, 1, 128))

    def ret_prev(h, i):
        row, rows, kk, to = pieces[i]
        src = snd.at[h, :, pl.ds(row, rows)]
        dst = rn.at[:, core * HALF + h, pl.ds(to, rows)]
        return remote(src, dst, s_rp.at[h, i], r_rn.at[h, core, i // 2], prev_dev(kk))

    def ret_next(h):
        src = snd.at[h, :, pl.ds(OWN_END, CUT)]
        dst = rp.at[:, core * HALF + h]
        return remote(src, dst, s_rn.at[h], r_rp.at[h, core], next_dev(0))

    def ret_up(h):
        return remote(up_snd.at[h], rp2.at[:, core * HALF + h], s_up.at[h], r_up.at[h, core], next_dev(0))

    def ret_sib(h):
        rows = pl.ds(pl.multiple_of(BACK + other * TOK, 128), TOK)
        return remote(snd.at[h, :, rows], rs.at[h], s_rs.at[0, h], r_rs.at[0, h], sib_dev)

    def ret_sib_q(h):
        rows = pl.ds(pl.multiple_of(other * TOK, TOK), TOK)
        return remote(dq_snd.at[h, rows], rs_q.at[h], s_rs.at[1, h], r_rs.at[1, h], sib_dev)

    def dots_prev(kk):
        return remote(e_sum, e_rcv.at[1 + core], s_e.at[kk], r_e.at[1 + core], prev_dev(kk))

    def dots_sib():
        return remote(e_sum, e_rcv.at[0], s_e.at[2], r_e.at[0], sib_dev)

    def dots_next():
        return remote(e_sum, e_rcv.at[3 + core], s_e.at[3], r_e.at[3 + core], next_dev(0))

    def dots_x(d):
        return remote(e_snd, e_x.at[d], s_x.at[1, d], r_x.at[1, d], x_devs[d])

    def pack(h, row, rows):
        snd[h, 0, row : row + rows] = dv_acc[row : row + rows].astype(BF)
        snd[h, 1, row : row + rows] = (dk_acc[row : row + rows] * scale).astype(BF)

    def add_dots(h, row, rows):
        at = slice(row, row + rows)
        ek[at] = ek[at] + dk_acc[at] * kw[h, at].astype(F32)

    def leave_first(h):
        pack(h, 0, 384)

        @pl.when(has_prev)
        def _():
            ret_prev(h, 0).start()
            ret_prev(h, 1).start()

        add_dots(h, 0, 384)

    def leave_last(h):
        add_dots(h, 384, SPAN - 384)

        @pl.when(h == HALF - 1)
        def _():
            row = lanes_sum_row(ek[...]) * scale
            row_q = lanes_sum_row(eq[...])
            e_snd[0:1, 128:TOK] = row[:, 0:256]
            for c in range(1, 5):
                e_snd[c : c + 1] = row[:, c * TOK - 128 : (c + 1) * TOK - 128]
            for c in range(2):
                e_snd[5 + c : 6 + c] = row_q[:, c * TOK : (c + 1) * TOK]
            e_snd[7:8, 0:256] = row_q[:, PAIR:ROWS_Q]
            for d in range(nx - 1):
                dots_x(d).start()

        pack(h, 384, SPAN - 384)
        up_snd[h, 0] = jnp.where(early_right, dq_snd[h, PAIR : PAIR + CUT], snd[h, 0, OWN_END + CUT : SPAN])
        up_snd[h, 1] = snd[h, 1, OWN_END + CUT : SPAN]

        @pl.when(has_prev)
        def _():
            ret_prev(h, 2).start()

        @pl.when(has_next)
        def _():
            ret_next(h).start()
            ret_up(h).start()

        ret_sib(h).start()
        ret_sib_q(h).start()

        @pl.when(h == HALF - 1)
        def _():
            total = e_snd[...]
            for d in range(nx - 1):
                dots_x(d).wait()
                total = total + e_x[d]
            e_sum[...] = total

            @pl.when(has_prev)
            def _():
                for kk in range(2):
                    dots_prev(kk).start()

            @pl.when(has_next)
            def _():
                dots_next().start()

            dots_sib().start()

    def inv_next_done(kk):
        return remote(i_snd, i_rcv.at[kk], s_i.at[kk], r_i.at[kk], prev_dev(kk))

    def inv_prev_done():
        return remote(i_snd, i_rcv.at[2], s_i.at[2], r_i.at[2], next_dev(0))

    def scores(h, t, at):
        q_rows = qw[h, t * QT : (t + 1) * QT]
        q_t = q_rows.T
        top = jnp.full((8, QT), -3e38, F32)
        for j in range(tile_steps[t]):
            rows = slice(j * KC, (j + 1) * KC)
            keys = slice(tile_first[t] + j * KC, tile_first[t] + (j + 1) * KC)
            s = dot(kw[h, keys], q_t) + bias[t, rows]
            sbuf[at, rows] = s
            top = jnp.maximum(top, jnp.max(s.reshape(KC // 8, 8, QT), axis=0))
        return q_rows, jnp.max(top, axis=0, keepdims=True)

    def weigh(h, t, at, q_rows, top):
        d_rows = dw[h, t * QT : (t + 1) * QT]
        d_t = d_rows.T
        total = jnp.zeros((8, QT), F32)
        delta = jnp.zeros((8, QT), F32)
        for j in range(tile_steps[t]):
            rows = slice(j * KC, (j + 1) * KC)
            keys = slice(tile_first[t] + j * KC, tile_first[t] + (j + 1) * KC)
            p = jnp.exp2((sbuf[at, rows] - top) * (scale * log2e))
            dp = dot(vw[h, keys], d_t)
            pbuf[at, rows] = p
            sbuf[at, rows] = dp
            total = total + jnp.sum(p.reshape(KC // 8, 8, QT), axis=0)
            delta = delta + jnp.sum((p * dp).reshape(KC // 8, 8, QT), axis=0)
        total = 1.0 / jnp.sum(total, axis=0, keepdims=True)
        delta = jnp.sum(delta, axis=0, keepdims=True) * total
        inverse = active[t, 0:1] * total
        inv_full = row_to_full(inverse)
        q_r = (q_rows.astype(F32) * inv_full).astype(BF)
        d_r = (d_rows.astype(F32) * inv_full).astype(BF)
        return q_rows, q_r, d_r, delta, inverse

    def spread(h, t, at, q_rows, q_r, d_r, delta, inverse):
        dq_t = jnp.zeros((DH, QT), F32)
        for j in range(tile_steps[t]):
            rows = slice(j * KC, (j + 1) * KC)
            keys = slice(tile_first[t] + j * KC, tile_first[t] + (j + 1) * KC)
            p = pbuf[at, rows]
            ds = (p * (sbuf[at, rows] - delta)).astype(BF)
            dv_acc[keys] = dv_acc[keys] + dot(p.astype(BF), d_r)
            dk_acc[keys] = dk_acc[keys] + dot(ds, q_r)
            dq_t = dq_t + dot(kt[:, keys], ds)
        dq = (dq_t * (inverse * scale)).T
        here = slice(t * QT, (t + 1) * QT)
        dq_snd[h, here] = dq.astype(BF)
        eq[here] = eq[here] + dq * q_rows.astype(F32)

    def tiles(h, group):
        kept = [scores(h, t, at) for at, t in enumerate(group)]
        kept = [weigh(h, t, at, *kept[at]) for at, t in enumerate(group)]
        for at, t in enumerate(group):
            spread(h, t, at, *kept[at])

    def head(h, carry):
        @pl.when(has_prev)
        def _():
            for arr in range(2):
                for kk in range(2):
                    row, rows = ((BACK - TOK - CUT, CUT), (BACK - TOK, TOK))[kk]
                    at = (vw, kw)[arr].at[h, pl.ds(row, rows)]
                    remote(at, at, s_fn.at[arr, h, kk], r_fn.at[arr, h, kk], prev_dev(kk)).wait_recv()

        @pl.when(has_next)
        def _():
            for arr in range(2):
                at = (vw, kw)[arr].at[h, pl.ds(OWN_END, CUT)]
                remote(at, at, s_fp.at[arr, h, 0], r_fp.at[arr, h], next_dev(0)).wait_recv()
                at = two_rcv.at[h, arr]
                remote(at, at, s_two.at[arr, h, 0], r_two.at[arr, h], next_dev(0)).wait_recv()

        for ref, row in ((kw, OWN_END + CUT), (qw, PAIR)):
            ref[h, row : row + CUT] = two_rcv[h, 0]
        for ref, row in ((vw, OWN_END + CUT), (dw, PAIR)):
            ref[h, row : row + CUT] = two_rcv[h, 1]

        @pl.when(h == 0)
        def _():
            gain = kg_ref[pl.ds(core * HALF, 1), :]

            def normed(slot, row, here, rows):
                at = slice(row, row + rows)
                full = row_to_full(i_rcv[slot, 0:1])[here : here + rows]
                kw[0, at] = (kw[0, at].astype(F32) * full * gain).astype(BF)

            @pl.when(has_prev)
            def _():
                for kk in range(2):
                    inv_next_done(kk).wait_recv()
                normed(0, BACK - TOK - CUT, CUT, CUT)
                normed(1, BACK - TOK, 0, TOK)

            @pl.when(has_next)
            def _():
                inv_prev_done().wait_recv()
                normed(2, OWN_END, 0, CUT)

        for j in range(SPAN // KC):
            kt[:, j * KC : (j + 1) * KC] = kw[h, j * KC : (j + 1) * KC].T
        dk_acc[...] = jnp.zeros_like(dk_acc)
        dv_acc[...] = jnp.zeros_like(dv_acc)
        tiles(h, (0, 1))
        leave_first(h)
        tiles(h, (2, 3))
        leave_last(h)
        return carry

    ek[...] = jnp.zeros_like(ek)
    eq[...] = jnp.zeros_like(eq)
    lax.fori_loop(0, HALF, head, 0)

    for h in range(HALF):
        ret_sib(h).wait_recv()
        ret_sib_q(h).wait_recv()

    def from_next(h):
        for c in range(2):
            @pl.when(at_core(c, has_next))
            def _():
                for kk in range(2):
                    for i in ((0,), (1, 2))[c]:
                        _, rows, _, to = pieces[i]
                        at = rn.at[:, kk * HALF + h, pl.ds(to, rows)]
                        remote(at, at, s_rp.at[h, i], r_rn.at[h, kk, i // 2], next_dev(kk)).wait_recv()

    def from_prev(h):
        @pl.when(at_core(0, has_prev))
        def _():
            for kk in range(2):
                at = rp.at[:, kk * HALF + h]
                remote(at, at, s_rn.at[h], r_rp.at[h, kk], prev_dev(kk)).wait_recv()
                at = rp2.at[:, kk * HALF + h]
                remote(at, at, s_up.at[h], r_up.at[h, kk], prev_dev(kk)).wait_recv()

    def own_grads(h, sib):
        g = (other if sib else core) * HALF + h
        if sib:
            return g, rs[h, 0], rs[h, 1]
        return g, snd[h, 0, own_win], snd[h, 1, own_win]

    def gather(h):
        for sib in (False, True):
            g, pv, pk = own_grads(h, sib)
            pq = (rs_q[h] if sib else dq_snd[h, own]).astype(F32)
            pk = pk.astype(F32) + rn[1, g].astype(F32)
            pv = pv.astype(F32) + rn[0, g].astype(F32)
            gain_q = qg_ref[pl.ds(g, 1), :]
            gain_k = kg_ref[pl.ds(g, 1), :]
            mixed = rp2[0, g].astype(F32)
            gq[g, 0:CUT] = (pq[0:CUT] + jnp.where(early_left, mixed, 0.0)) * gain_q
            gq[g, CUT:TOK] = pq[CUT:TOK] * gain_q
            gk[g, 0:CUT] = (pk[0:CUT] + rp[1, g].astype(F32)) * gain_k
            gk[g, CUT:TOK] = (pk[CUT:TOK] + rp2[1, g].astype(F32)) * gain_k
            ov_ref[g, 0:CUT] = (pv[0:CUT] + rp[0, g].astype(F32)).astype(BF)
            ov_ref[g, CUT:TOK] = (pv[CUT:TOK] + jnp.where(early_left, 0.0, mixed)).astype(BF)

    for h in range(HALF):
        from_next(h)
        from_prev(h)
        gather(h)

    dots_sib().wait_recv()

    @pl.when(has_next)
    def _():
        for kk in range(2):
            at = e_rcv.at[1 + kk]
            remote(at, at, s_e.at[kk], r_e.at[1 + kk], next_dev(kk)).wait_recv()

    @pl.when(has_prev & (core == 0))
    def _():
        for kk in range(2):
            at = e_rcv.at[3 + kk]
            remote(at, at, s_e.at[3], r_e.at[3 + kk], prev_dev(kk)).wait_recv()

    dot_q = e_sum[pl.ds(5 + core, 1)] + e_rcv[0, pl.ds(5 + core, 1)] + (e_rcv[3, 7:8] + e_rcv[4, 7:8])
    dot_k = e_sum[pl.ds(2 + core, 1)] + e_rcv[0, pl.ds(2 + core, 1)]
    dot_k = dot_k + (e_rcv[1, pl.ds(core, 1)] + e_rcv[2, pl.ds(core, 1)]) + (e_rcv[3, 4:5] + e_rcv[4, 4:5])
    cq = invq[...] * invq[...] * row_to_full(dot_q / features)
    ck = invk[...] * invk[...] * row_to_full(dot_k / features)
    for g in range(LOC):
        oq_ref[g] = (invq[...] * gq[g] - qraw[g].astype(F32) * cq).astype(BF)

    def finish_k(h):
        for sib in (False, True):
            g = (other if sib else core) * HALF + h
            ok_ref[g] = (invk[...] * gk[g] - kraw[g].astype(F32) * ck).astype(BF)

    for h in range(HALF):
        finish_k(h)

    for c in to_sib:
        c.wait_send()

    @pl.when(has_next)
    def _():
        for h in range(HALF):
            ret_next(h).wait_send()
            ret_up(h).wait_send()
        dots_next().wait_send()
        for kk in range(2):
            inv_next(kk).wait_send()

    @pl.when(has_prev)
    def _():
        for h in range(HALF):
            for i in range(3):
                ret_prev(h, i).wait_send()
        for kk in range(2):
            dots_prev(kk).wait_send()

    @pl.when(has_prev & (core == 0))
    def _():
        for arr in range(2):
            for h in range(HALF):
                for kk in range(2):
                    fwd_prev(arr, h, kk).wait_send()
                    two_prev(arr, h, kk).wait_send()
        for kk in range(2):
            inv_prev(kk).wait_send()

    for c in range(2):
        @pl.when(at_core(c, has_next))
        def _():
            for arr in range(2):
                for h in range(HALF):
                    for kk in range(2):
                        fwd_next(arr, h, kk, c).wait_send()

    for h in range(HALF):
        ret_sib(h).wait_send()
        ret_sib_q(h).wait_send()
    dots_sib().wait_send()


def local(queries, keys, values, out_grads, query_gain, key_gain, block_lengths):
    nctx, nx = lax.axis_size("ctx"), lax.axis_size("head")
    heads_first = [jnp.moveaxis(a, 1, 0) for a in (queries, keys, values, out_grads)]
    big = (LOC, TOK, DH)
    dma = pltpu.SemaphoreType.DMA
    vmem = pltpu.VMEM
    out = jax.ShapeDtypeStruct(big, BF)
    any_spec = pl.BlockSpec(memory_space=pl.ANY)
    vmem_spec = pl.BlockSpec(memory_space=pltpu.VMEM)
    res = pl.pallas_call(
        functools.partial(body, nctx, nx),
        out_shape=(out, out, out),
        in_specs=[pl.BlockSpec(memory_space=pltpu.HBM)] * 7,
        out_specs=(vmem_spec, vmem_spec, vmem_spec),
        scratch_shapes=[
            vmem((LOC, DH), F32), vmem((LOC, DH), F32), vmem((1, block_lengths.shape[0]), jnp.int32),
            vmem(big, BF), vmem(big, BF), vmem((LOC, CUT, DH), BF), vmem((LOC, CUT, DH), BF), vmem(big, BF), vmem(big, BF),
            vmem((HALF, SPAN, DH), BF), vmem((HALF, SPAN, DH), BF),
            vmem((HALF, ROWS_Q, DH), BF), vmem((HALF, ROWS_Q, DH), BF),
            vmem((LOC, 2, CUT, DH), BF), vmem((HALF, 2, CUT, DH), BF),
            vmem((TOK, DH), F32), vmem((TOK, DH), F32),
            vmem((8, TOK), F32), vmem((nx - 1, 8, TOK), F32),
            vmem((NQ, WIN, QT), F32), vmem((NQ, 8, QT), F32), vmem((2, WIN, QT), F32), vmem((2, WIN, QT), F32),
            vmem((DH, SPAN), BF), vmem((SPAN, DH), F32), vmem((SPAN, DH), F32),
            vmem((SPAN, DH), F32), vmem((ROWS_Q, DH), F32), vmem((8, TOK), F32), vmem((nx - 1, 8, TOK), F32),
            vmem((8, TOK), F32), vmem((5, 8, TOK), F32),
            vmem((8, TOK), F32), vmem((3, 8, TOK), F32),
            vmem((HALF, 2, SPAN, DH), BF), vmem((HALF, ROWS_Q, DH), BF), vmem((HALF, 2, CUT, DH), BF),
            vmem((2,) + big, BF), vmem((2, LOC, CUT, DH), BF), vmem((2, LOC, CUT, DH), BF), vmem((HALF, 2, TOK, DH), BF), vmem((HALF, TOK, DH), BF),
            vmem(big, F32), vmem(big, F32),
            dma((11,)),
            dma((2, HALF, 2)), dma((2, HALF, 2)), dma((2, HALF, 2)), dma((2, HALF)),
            dma((4,)), dma((4,)), dma((2, 3)), dma((2, 3)),
            dma((HALF, 3)), dma((HALF, 2, 2)), dma((HALF,)), dma((HALF, 2)),
            dma((2, HALF)), dma((2, HALF)), dma((4,)), dma((5,)), dma((4,)), dma((3,)),
            dma((2, HALF, 2)), dma((2, HALF)), dma((HALF,)), dma((HALF, 2)),
        ],
        compiler_params=pltpu.CompilerParams(
            collective_id=0, has_side_effects=True, vmem_limit_bytes=52 << 20
        ),
    )(*heads_first, query_gain, key_gain, block_lengths.reshape(1, -1))
    return tuple(jnp.moveaxis(a, 0, 1) for a in res)


def solution(mesh):
    placed = (
        P("ctx", "head", None),
        P("ctx", "head", None),
        P("ctx", "head", None),
        P("ctx", "head", None),
        P("head", None),
        P("head", None),
        P(),
    )
    return jax.shard_map(
        local,
        mesh=mesh,
        in_specs=placed,
        out_specs=(P("ctx", "head", None), P("ctx", "head", None), P("ctx", "head", None)),
        check_vma=False,
    )
```

```python
import functools

import jax
import jax.numpy as jnp
from jax import lax
from jax.experimental import pallas as pl
from jax.experimental.pallas import tpu as pltpu
from jax.sharding import PartitionSpec as P

MESH = pl.DeviceIdType.MESH
norm_eps = 1e-06
hidden = -1e30
BF = jnp.bfloat16
F32 = jnp.float32

TOK = 384
PAIR = 2 * TOK
CUT = TOK // 2
BACK = 640
OWN_END = BACK + PAIR
SPAN = OWN_END + TOK
LOC = 6
HALF = 3
DH = 128
QT = 256
NQ = PAIR // QT + 1
ROWS_Q = NQ * QT
WIN = 1408
KC = 128
NK = WIN // KC
tile_first = (0, 128, 384, 640)
tile_steps = (NK - 1, NK, NK, 8)


def dot(a, b):
    return jnp.dot(a, b, preferred_element_type=F32)


def lanes_sum_row(x):
    return jnp.sum(x.T, axis=0, keepdims=True)


def row_to_full(row):
    return jnp.broadcast_to(row, (DH, row.shape[1])).T


def body(
    nctx, nx,
    q_hbm, k_hbm, v_hbm, d_hbm, qg_hbm, kg_hbm, len_hbm,
    oq_ref, ok_ref, ov_ref,
    qg_ref, kg_ref, len_ref, qraw, kraw, vhalf, dhalf, qn, kn, kw, vw, qw, dw, two_snd, two_rcv,
    invq, invk, st_a, st_b,
    bias, active, sbuf, pbuf, kt, dk_acc, dv_acc, ek, eq, e_snd, e_x, e_sum, e_rcv, i_snd, i_rcv,
    snd, dq_snd, up_snd, rn, rp, rp2, rs, rs_q, gq, gk,
    lsem, s_fn, r_fn, s_fp, r_fp, s_sib, r_sib, s_x, r_x, s_rp, r_rn, s_rn, r_rp, s_rs, r_rs, s_e, r_e, s_i, r_i, s_two, r_two, s_up, r_up,
):
    me = lax.axis_index("ctx")
    x = lax.axis_index("head")
    core = lax.rem(me, 2)
    chip = me // 2
    chips = nctx // 2
    has_prev = chip > 0
    has_next = chip < chips - 1
    other = 1 - core
    features = float(nx * LOC * DH)
    scale = DH ** -0.5
    log2e = 1.4426950408889634
    sib_dev = (2 * chip + other, x)
    x_devs = [(me, lax.rem(x + d, nx)) for d in range(1, nx)]

    def next_dev(kk):
        return (2 * chip + 2 + kk, x)

    def prev_dev(kk):
        return (2 * chip - 2 + kk, x)

    def remote(src, dst, ss, rs_, dev):
        return pltpu.make_async_remote_copy(
            src_ref=src, dst_ref=dst, send_sem=ss, recv_sem=rs_, device_id=dev, device_id_type=MESH
        )

    bar = pltpu.get_barrier_semaphore()

    @pl.when(has_next)
    def _():
        for kk in range(2):
            pl.semaphore_signal(bar, inc=1, device_id=next_dev(kk), device_id_type=MESH)

    @pl.when(has_prev)
    def _():
        for kk in range(2):
            pl.semaphore_signal(bar, inc=1, device_id=prev_dev(kk), device_id_type=MESH)

    pl.semaphore_signal(bar, inc=1, device_id=sib_dev, device_id_type=MESH)
    for dev in x_devs:
        pl.semaphore_signal(bar, inc=1, device_id=dev, device_id_type=MESH)

    own = pl.ds(pl.multiple_of(core * TOK, TOK), TOK)
    own_win = pl.ds(pl.multiple_of(BACK + core * TOK, 128), TOK)
    own_heads = pl.ds(core * HALF, HALF)
    sib_heads = pl.ds(other * HALF, HALF)
    load_k = pltpu.make_async_copy(k_hbm, kraw, lsem.at[0])
    load_q = pltpu.make_async_copy(q_hbm, qraw, lsem.at[1])
    self_v = pltpu.make_async_copy(v_hbm.at[own_heads], vw.at[:, own_win], lsem.at[2])
    self_d = pltpu.make_async_copy(d_hbm.at[own_heads], dw.at[:, own], lsem.at[3])
    load_small = [
        pltpu.make_async_copy(qg_hbm, qg_ref, lsem.at[6]),
        pltpu.make_async_copy(kg_hbm, kg_ref, lsem.at[7]),
        pltpu.make_async_copy(len_hbm, len_ref, lsem.at[8]),
    ]
    load_vh = pltpu.make_async_copy(v_hbm.at[:, pl.ds(CUT, CUT)], vhalf, lsem.at[9])
    load_dh = pltpu.make_async_copy(d_hbm.at[:, pl.ds(0, CUT)], dhalf, lsem.at[10])
    load_k.start()
    load_q.start()
    self_v.start()
    self_d.start()
    for c in load_small:
        c.start()
    load_vh.start()
    load_dh.start()

    @pl.when(has_prev & has_next)
    def _():
        pl.semaphore_wait(bar, nx + 4)

    @pl.when(jnp.logical_not(has_prev & has_next))
    def _():
        pl.semaphore_wait(bar, nx + 2)

    def fwd_next(arr, h, kk, c):
        src = (v_hbm, kn if h else k_hbm)[arr].at[kk * HALF + h]
        if c == 0:
            src = src.at[pl.ds(CUT, CUT)]
            dst = (vw, kw)[arr].at[h, pl.ds(BACK - TOK - CUT, CUT)]
        else:
            dst = (vw, kw)[arr].at[h, pl.ds(BACK - TOK, TOK)]
        return remote(src, dst, s_fn.at[arr, h, kk], r_fn.at[arr, h, c], next_dev(kk))

    def fwd_prev(arr, h, kk):
        src = (v_hbm, kn if h else k_hbm)[arr].at[kk * HALF + h, pl.ds(0, CUT)]
        dst = (vw, kw)[arr].at[h, pl.ds(OWN_END, CUT)]
        return remote(src, dst, s_fp.at[arr, h, kk], r_fp.at[arr, h], prev_dev(kk))

    def two_prev(arr, h, kk):
        return remote(
            two_snd.at[kk * HALF + h, arr], two_rcv.at[h, arr], s_two.at[arr, h, kk], r_two.at[arr, h], prev_dev(kk)
        )

    def at_core(c, cond):
        return cond & (core == c)

    def go_next(arr, h):
        for c in range(2):
            @pl.when(at_core(c, has_next))
            def _():
                for kk in range(2):
                    fwd_next(arr, h, kk, c).start()

    def go_prev(arr, h):
        @pl.when(at_core(0, has_prev))
        def _():
            for kk in range(2):
                fwd_prev(arr, h, kk).start()

    def go_two(arr, h):
        @pl.when(at_core(0, has_prev))
        def _():
            for kk in range(2):
                two_prev(arr, h, kk).start()

    to_sib = [
        remote(v_hbm.at[sib_heads], vw.at[:, own_win], s_sib.at[0], r_sib.at[0], sib_dev),
        remote(d_hbm.at[sib_heads], dw.at[:, own], s_sib.at[1], r_sib.at[1], sib_dev),
        remote(kn.at[sib_heads], kw.at[:, own_win], s_sib.at[2], r_sib.at[2], sib_dev),
        remote(qn.at[sib_heads], qw.at[:, own], s_sib.at[3], r_sib.at[3], sib_dev),
    ]
    go_next(0, 0)
    go_prev(0, 0)
    go_next(1, 0)
    go_prev(1, 0)
    go_prev(0, 1)
    go_prev(0, 2)
    to_sib[0].start()
    to_sib[1].start()

    def sum_start(rows, mine, theirs, rnd):
        mine[0:1, :] = rows[0]
        mine[1:2, :] = rows[1]
        copies = [
            remote(mine, theirs.at[d], s_x.at[rnd, d], r_x.at[rnd, d], x_devs[d]) for d in range(nx - 1)
        ]
        for c in copies:
            c.start()
        return copies

    def sum_done(copies, mine, theirs):
        for c in copies:
            c.wait()
        total = mine[0:2, :]
        for d in range(nx - 1):
            total = total + theirs[d, 0:2, :]
        return total[0:1, :], total[1:2, :]

    def inv_next(kk):
        return remote(i_snd, i_rcv.at[core], s_i.at[kk], r_i.at[core], next_dev(kk))

    def inv_prev(kk):
        return remote(i_snd, i_rcv.at[2], s_i.at[2 + kk], r_i.at[2], prev_dev(kk))

    def squares(ref):
        total = jnp.zeros((TOK, DH), F32)
        for g in range(LOC):
            v = ref[g].astype(F32)
            total = total + v * v
        return lanes_sum_row(total)

    load_q.wait()
    load_k.wait()
    for small in (st_a, e_snd, e_rcv, i_snd):
        small[...] = jnp.zeros_like(small)
    squares_x = sum_start((squares(qraw), squares(kraw)), st_a, st_b, 0)
    for c in load_small:
        c.wait()
    nb = len_ref.shape[1]
    lens = len_ref[...].astype(F32)
    ri = lax.broadcasted_iota(jnp.int32, (nb, nb), 0)
    ci = lax.broadcasted_iota(jnp.int32, (nb, nb), 1)
    ends_col = jnp.sum(jnp.where(ci <= ri, lens, 0.0), axis=1, keepdims=True)
    left = (chip * PAIR).astype(F32)
    right = left + PAIR

    def block_end(edge):
        after = jnp.where(ends_col >= edge, ends_col, 1e9) + jnp.zeros((1, DH), F32)
        return jnp.min(after, axis=0, keepdims=True)

    end_left = jnp.where(chip > 0, block_end(left), 0.0)
    end_right = block_end(right)
    early_left = end_left - left <= CUT
    early_right = end_right - right <= CUT
    load_vh.wait()
    load_dh.wait()
    for g in range(LOC):
        two_snd[g, 1] = jnp.where(early_left, dhalf[g], vhalf[g])
    go_two(1, 0)
    go_two(1, 1)
    for h in range(HALF):
        kw[h, 0 : BACK - TOK - CUT] = jnp.zeros((BACK - TOK - CUT, DH), BF)
        vw[h, 0 : BACK - TOK - CUT] = jnp.zeros((BACK - TOK - CUT, DH), BF)
        qw[h, PAIR + CUT : ROWS_Q] = jnp.zeros((ROWS_Q - PAIR - CUT, DH), BF)
        dw[h, PAIR + CUT : ROWS_Q] = jnp.zeros((ROWS_Q - PAIR - CUT, DH), BF)

    @pl.when(jnp.logical_not(has_prev))
    def _():
        for h in range(HALF):
            kw[h, BACK - TOK - CUT : BACK] = jnp.zeros((TOK + CUT, DH), BF)
            vw[h, BACK - TOK - CUT : BACK] = jnp.zeros((TOK + CUT, DH), BF)

    @pl.when(jnp.logical_not(has_next))
    def _():
        for h in range(HALF):
            kw[h, OWN_END : OWN_END + CUT] = jnp.zeros((CUT, DH), BF)
            vw[h, OWN_END : OWN_END + CUT] = jnp.zeros((CUT, DH), BF)
        two_rcv[...] = jnp.zeros_like(two_rcv)
        rn[...] = jnp.zeros_like(rn)

    @pl.when(at_core(0, has_next))
    def _():
        rn[:, :, 0:CUT] = jnp.zeros((2, LOC, CUT, DH), BF)

    @pl.when(jnp.logical_not(at_core(0, has_prev)))
    def _():
        rp[...] = jnp.zeros_like(rp)
        rp2[...] = jnp.zeros_like(rp2)

    first_pos = chip * PAIR - BACK
    pos = (first_pos + lax.broadcasted_iota(jnp.int32, (1, SPAN), 1)).astype(F32)
    blocks = jnp.sum(jnp.where(ends_col <= pos, 1.0, 0.0), axis=0, keepdims=True)
    q_pos = pos[:, BACK : BACK + ROWS_Q]
    q_block = blocks[:, BACK : BACK + ROWS_Q]
    k_block = jnp.where(pos >= 0.0, blocks, -10.0)
    k_full = row_to_full(k_block)
    for t in range(NQ):
        at, rows = tile_first[t], tile_steps[t] * KC
        kb = k_full[at : at + rows]
        for c in range(QT // DH):
            lanes = slice(c * DH, (c + 1) * DH)
            here = slice(t * QT + c * DH, t * QT + (c + 1) * DH)
            qb = q_block[:, here]
            seen = (kb <= qb) & (kb >= qb - 1.0)
            bias[t, 0:rows, lanes] = jnp.where(seen, 0.0, hidden)
            if t < NQ - 1:
                away = jnp.where(early_left, end_left, 0.0)
                computed = jnp.where(q_pos[:, here] >= away, 1.0, 0.0)
            else:
                until = jnp.where(early_right, end_right, 0.0)
                computed = jnp.where(q_pos[:, here] < until, 1.0, 0.0)
            active[t, 0:1, lanes] = computed

    sum_q, sum_k = sum_done(squares_x, st_a, st_b)
    row_invk = lax.rsqrt(sum_k / features + norm_eps)
    i_snd[0:1] = row_invk

    @pl.when(has_next)
    def _():
        for kk in range(2):
            inv_next(kk).start()

    @pl.when(has_prev & (core == 0))
    def _():
        for kk in range(2):
            inv_prev(kk).start()

    go_next(0, 1)
    invk[...] = row_to_full(row_invk)
    invq[...] = row_to_full(lax.rsqrt(sum_q / features + norm_eps))
    for h in range(HALF):
        for kk in range(2):
            g = kk * HALF + h
            kn[g] = (kraw[g].astype(F32) * invk[...] * kg_ref[g : g + 1, :]).astype(BF)
            qn[g] = (qraw[g].astype(F32) * invq[...] * qg_ref[g : g + 1, :]).astype(BF)
            two_snd[g, 0] = jnp.where(early_left, qn[g, 0:CUT], kn[g, CUT:TOK])
        if h:
            go_next(1, h)
            if h > 1:
                go_next(0, h)
            go_prev(1, h)
        go_two(0, h)
    go_two(1, 2)
    to_sib[2].start()
    to_sib[3].start()
    self_k = pltpu.make_async_copy(kn.at[own_heads], kw.at[:, own_win], lsem.at[4])
    self_q = pltpu.make_async_copy(qn.at[own_heads], qw.at[:, own], lsem.at[5])
    self_k.start()
    self_q.start()

    self_v.wait()
    self_d.wait()
    self_k.wait()
    self_q.wait()
    for c in to_sib:
        c.wait_recv()

    pieces = ((64, 192, 0, 192), (256, 128, 1, 0), (384, 256, 1, 128))

    def ret_prev(h, i):
        row, rows, kk, to = pieces[i]
        src = snd.at[h, :, pl.ds(row, rows)]
        dst = rn.at[:, core * HALF + h, pl.ds(to, rows)]
        return remote(src, dst, s_rp.at[h, i], r_rn.at[h, core, i // 2], prev_dev(kk))

    def ret_next(h):
        src = snd.at[h, :, pl.ds(OWN_END, CUT)]
        dst = rp.at[:, core * HALF + h]
        return remote(src, dst, s_rn.at[h], r_rp.at[h, core], next_dev(0))

    def ret_up(h):
        return remote(up_snd.at[h], rp2.at[:, core * HALF + h], s_up.at[h], r_up.at[h, core], next_dev(0))

    def ret_sib(h):
        rows = pl.ds(pl.multiple_of(BACK + other * TOK, 128), TOK)
        return remote(snd.at[h, :, rows], rs.at[h], s_rs.at[0, h], r_rs.at[0, h], sib_dev)

    def ret_sib_q(h):
        rows = pl.ds(pl.multiple_of(other * TOK, TOK), TOK)
        return remote(dq_snd.at[h, rows], rs_q.at[h], s_rs.at[1, h], r_rs.at[1, h], sib_dev)

    def dots_prev(kk):
        return remote(e_sum, e_rcv.at[1 + core], s_e.at[kk], r_e.at[1 + core], prev_dev(kk))

    def dots_sib():
        return remote(e_sum, e_rcv.at[0], s_e.at[2], r_e.at[0], sib_dev)

    def dots_next():
        return remote(e_sum, e_rcv.at[3 + core], s_e.at[3], r_e.at[3 + core], next_dev(0))

    def dots_x(d):
        return remote(e_snd, e_x.at[d], s_x.at[1, d], r_x.at[1, d], x_devs[d])

    def pack(h, row, rows):
        snd[h, 0, row : row + rows] = dv_acc[row : row + rows].astype(BF)
        snd[h, 1, row : row + rows] = (dk_acc[row : row + rows] * scale).astype(BF)

    def add_dots(h, row, rows):
        at = slice(row, row + rows)
        ek[at] = ek[at] + dk_acc[at] * kw[h, at].astype(F32)

    def leave_first(h):
        pack(h, 0, 384)

        @pl.when(has_prev)
        def _():
            ret_prev(h, 0).start()
            ret_prev(h, 1).start()

        add_dots(h, 0, 384)

    def leave_last(h):
        add_dots(h, 384, SPAN - 384)

        @pl.when(h == HALF - 1)
        def _():
            row = lanes_sum_row(ek[...]) * scale
            row_q = lanes_sum_row(eq[...])
            e_snd[0:1, 128:TOK] = row[:, 0:256]
            for c in range(1, 5):
                e_snd[c : c + 1] = row[:, c * TOK - 128 : (c + 1) * TOK - 128]
            for c in range(2):
                e_snd[5 + c : 6 + c] = row_q[:, c * TOK : (c + 1) * TOK]
            e_snd[7:8, 0:256] = row_q[:, PAIR:ROWS_Q]
            for d in range(nx - 1):
                dots_x(d).start()

        pack(h, 384, SPAN - 384)
        up_snd[h, 0] = jnp.where(early_right, dq_snd[h, PAIR : PAIR + CUT], snd[h, 0, OWN_END + CUT : SPAN])
        up_snd[h, 1] = snd[h, 1, OWN_END + CUT : SPAN]

        @pl.when(has_prev)
        def _():
            ret_prev(h, 2).start()

        @pl.when(has_next)
        def _():
            ret_next(h).start()
            ret_up(h).start()

        ret_sib(h).start()
        ret_sib_q(h).start()

        @pl.when(h == HALF - 1)
        def _():
            total = e_snd[...]
            for d in range(nx - 1):
                dots_x(d).wait()
                total = total + e_x[d]
            e_sum[...] = total

            @pl.when(has_prev)
            def _():
                for kk in range(2):
                    dots_prev(kk).start()

            @pl.when(has_next)
            def _():
                dots_next().start()

            dots_sib().start()

    def inv_next_done(kk):
        return remote(i_snd, i_rcv.at[kk], s_i.at[kk], r_i.at[kk], prev_dev(kk))

    def inv_prev_done():
        return remote(i_snd, i_rcv.at[2], s_i.at[2], r_i.at[2], next_dev(0))

    def scores(h, t, at):
        q_rows = qw[h, t * QT : (t + 1) * QT]
        q_t = q_rows.T
        top = jnp.full((8, QT), -3e38, F32)
        for j in range(tile_steps[t]):
            rows = slice(j * KC, (j + 1) * KC)
            keys = slice(tile_first[t] + j * KC, tile_first[t] + (j + 1) * KC)
            s = dot(kw[h, keys], q_t) + bias[t, rows]
            sbuf[at, rows] = s
            top = jnp.maximum(top, jnp.max(s.reshape(KC // 8, 8, QT), axis=0))
        return q_rows, jnp.max(top, axis=0, keepdims=True)

    def weigh(h, t, at, q_rows, top):
        d_rows = dw[h, t * QT : (t + 1) * QT]
        d_t = d_rows.T
        total = jnp.zeros((8, QT), F32)
        delta = jnp.zeros((8, QT), F32)
        for j in range(tile_steps[t]):
            rows = slice(j * KC, (j + 1) * KC)
            keys = slice(tile_first[t] + j * KC, tile_first[t] + (j + 1) * KC)
            p = jnp.exp2((sbuf[at, rows] - top) * (scale * log2e))
            dp = dot(vw[h, keys], d_t)
            pbuf[at, rows] = p
            sbuf[at, rows] = dp
            total = total + jnp.sum(p.reshape(KC // 8, 8, QT), axis=0)
            delta = delta + jnp.sum((p * dp).reshape(KC // 8, 8, QT), axis=0)
        total = 1.0 / jnp.sum(total, axis=0, keepdims=True)
        delta = jnp.sum(delta, axis=0, keepdims=True) * total
        inverse = active[t, 0:1] * total
        inv_full = row_to_full(inverse)
        q_r = (q_rows.astype(F32) * inv_full).astype(BF)
        d_r = (d_rows.astype(F32) * inv_full).astype(BF)
        return q_rows, q_r, d_r, delta, inverse

    def spread(h, t, at, q_rows, q_r, d_r, delta, inverse):
        dq_t = jnp.zeros((DH, QT), F32)
        for j in range(tile_steps[t]):
            rows = slice(j * KC, (j + 1) * KC)
            keys = slice(tile_first[t] + j * KC, tile_first[t] + (j + 1) * KC)
            p = pbuf[at, rows]
            ds = (p * (sbuf[at, rows] - delta)).astype(BF)
            dv_acc[keys] = dv_acc[keys] + dot(p.astype(BF), d_r)
            dk_acc[keys] = dk_acc[keys] + dot(ds, q_r)
            dq_t = dq_t + dot(kt[:, keys], ds)
        dq = (dq_t * (inverse * scale)).T
        here = slice(t * QT, (t + 1) * QT)
        dq_snd[h, here] = dq.astype(BF)
        eq[here] = eq[here] + dq * q_rows.astype(F32)

    def tiles(h, group):
        kept = [scores(h, t, at) for at, t in enumerate(group)]
        kept = [weigh(h, t, at, *kept[at]) for at, t in enumerate(group)]
        for at, t in enumerate(group):
            spread(h, t, at, *kept[at])

    def head(h, carry):
        @pl.when(has_prev)
        def _():
            for arr in range(2):
                for kk in range(2):
                    row, rows = ((BACK - TOK - CUT, CUT), (BACK - TOK, TOK))[kk]
                    at = (vw, kw)[arr].at[h, pl.ds(row, rows)]
                    remote(at, at, s_fn.at[arr, h, kk], r_fn.at[arr, h, kk], prev_dev(kk)).wait_recv()

        @pl.when(has_next)
        def _():
            for arr in range(2):
                at = (vw, kw)[arr].at[h, pl.ds(OWN_END, CUT)]
                remote(at, at, s_fp.at[arr, h, 0], r_fp.at[arr, h], next_dev(0)).wait_recv()
                at = two_rcv.at[h, arr]
                remote(at, at, s_two.at[arr, h, 0], r_two.at[arr, h], next_dev(0)).wait_recv()

        for ref, row in ((kw, OWN_END + CUT), (qw, PAIR)):
            ref[h, row : row + CUT] = two_rcv[h, 0]
        for ref, row in ((vw, OWN_END + CUT), (dw, PAIR)):
            ref[h, row : row + CUT] = two_rcv[h, 1]

        @pl.when(h == 0)
        def _():
            gain = kg_ref[pl.ds(core * HALF, 1), :]

            def normed(slot, row, here, rows):
                at = slice(row, row + rows)
                full = row_to_full(i_rcv[slot, 0:1])[here : here + rows]
                kw[0, at] = (kw[0, at].astype(F32) * full * gain).astype(BF)

            @pl.when(has_prev)
            def _():
                for kk in range(2):
                    inv_next_done(kk).wait_recv()
                normed(0, BACK - TOK - CUT, CUT, CUT)
                normed(1, BACK - TOK, 0, TOK)

            @pl.when(has_next)
            def _():
                inv_prev_done().wait_recv()
                normed(2, OWN_END, 0, CUT)

        for j in range(SPAN // KC):
            kt[:, j * KC : (j + 1) * KC] = kw[h, j * KC : (j + 1) * KC].T
        dk_acc[...] = jnp.zeros_like(dk_acc)
        dv_acc[...] = jnp.zeros_like(dv_acc)
        tiles(h, (0, 1))
        leave_first(h)
        tiles(h, (2, 3))
        leave_last(h)
        return carry

    ek[...] = jnp.zeros_like(ek)
    eq[...] = jnp.zeros_like(eq)
    lax.fori_loop(0, HALF, head, 0)

    for h in range(HALF):
        ret_sib(h).wait_recv()
        ret_sib_q(h).wait_recv()

    def from_next(h):
        for c in range(2):
            @pl.when(at_core(c, has_next))
            def _():
                for kk in range(2):
                    for i in ((0,), (1, 2))[c]:
                        _, rows, _, to = pieces[i]
                        at = rn.at[:, kk * HALF + h, pl.ds(to, rows)]
                        remote(at, at, s_rp.at[h, i], r_rn.at[h, kk, i // 2], next_dev(kk)).wait_recv()

    def from_prev(h):
        @pl.when(at_core(0, has_prev))
        def _():
            for kk in range(2):
                at = rp.at[:, kk * HALF + h]
                remote(at, at, s_rn.at[h], r_rp.at[h, kk], prev_dev(kk)).wait_recv()
                at = rp2.at[:, kk * HALF + h]
                remote(at, at, s_up.at[h], r_up.at[h, kk], prev_dev(kk)).wait_recv()

    def own_grads(h, sib):
        g = (other if sib else core) * HALF + h
        if sib:
            return g, rs[h, 0], rs[h, 1]
        return g, snd[h, 0, own_win], snd[h, 1, own_win]

    def gather(h):
        for sib in (False, True):
            g, pv, pk = own_grads(h, sib)
            pq = (rs_q[h] if sib else dq_snd[h, own]).astype(F32)
            pk = pk.astype(F32) + rn[1, g].astype(F32)
            pv = pv.astype(F32) + rn[0, g].astype(F32)
            gain_q = qg_ref[pl.ds(g, 1), :]
            gain_k = kg_ref[pl.ds(g, 1), :]
            mixed = rp2[0, g].astype(F32)
            gq[g, 0:CUT] = (pq[0:CUT] + jnp.where(early_left, mixed, 0.0)) * gain_q
            gq[g, CUT:TOK] = pq[CUT:TOK] * gain_q
            gk[g, 0:CUT] = (pk[0:CUT] + rp[1, g].astype(F32)) * gain_k
            gk[g, CUT:TOK] = (pk[CUT:TOK] + rp2[1, g].astype(F32)) * gain_k
            ov_ref[g, 0:CUT] = (pv[0:CUT] + rp[0, g].astype(F32)).astype(BF)
            ov_ref[g, CUT:TOK] = (pv[CUT:TOK] + jnp.where(early_left, 0.0, mixed)).astype(BF)

    for h in range(HALF):
        from_next(h)
        from_prev(h)
        gather(h)

    dots_sib().wait_recv()

    @pl.when(has_next)
    def _():
        for kk in range(2):
            at = e_rcv.at[1 + kk]
            remote(at, at, s_e.at[kk], r_e.at[1 + kk], next_dev(kk)).wait_recv()

    @pl.when(has_prev & (core == 0))
    def _():
        for kk in range(2):
            at = e_rcv.at[3 + kk]
            remote(at, at, s_e.at[3], r_e.at[3 + kk], prev_dev(kk)).wait_recv()

    dot_q = e_sum[pl.ds(5 + core, 1)] + e_rcv[0, pl.ds(5 + core, 1)] + (e_rcv[3, 7:8] + e_rcv[4, 7:8])
    dot_k = e_sum[pl.ds(2 + core, 1)] + e_rcv[0, pl.ds(2 + core, 1)]
    dot_k = dot_k + (e_rcv[1, pl.ds(core, 1)] + e_rcv[2, pl.ds(core, 1)]) + (e_rcv[3, 4:5] + e_rcv[4, 4:5])
    cq = invq[...] * invq[...] * row_to_full(dot_q / features)
    ck = invk[...] * invk[...] * row_to_full(dot_k / features)
    for g in range(LOC):
        oq_ref[g] = (invq[...] * gq[g] - qraw[g].astype(F32) * cq).astype(BF)

    def finish_k(h):
        for sib in (False, True):
            g = (other if sib else core) * HALF + h
            ok_ref[g] = (invk[...] * gk[g] - kraw[g].astype(F32) * ck).astype(BF)

    for h in range(HALF):
        finish_k(h)

    for c in to_sib:
        c.wait_send()

    @pl.when(has_next)
    def _():
        for h in range(HALF):
            ret_next(h).wait_send()
            ret_up(h).wait_send()
        dots_next().wait_send()
        for kk in range(2):
            inv_next(kk).wait_send()

    @pl.when(has_prev)
    def _():
        for h in range(HALF):
            for i in range(3):
                ret_prev(h, i).wait_send()
        for kk in range(2):
            dots_prev(kk).wait_send()

    @pl.when(has_prev & (core == 0))
    def _():
        for arr in range(2):
            for h in range(HALF):
                for kk in range(2):
                    fwd_prev(arr, h, kk).wait_send()
                    two_prev(arr, h, kk).wait_send()
        for kk in range(2):
            inv_prev(kk).wait_send()

    for c in range(2):
        @pl.when(at_core(c, has_next))
        def _():
            for arr in range(2):
                for h in range(HALF):
                    for kk in range(2):
                        fwd_next(arr, h, kk, c).wait_send()

    for h in range(HALF):
        ret_sib(h).wait_send()
        ret_sib_q(h).wait_send()
    dots_sib().wait_send()


def local(queries, keys, values, out_grads, query_gain, key_gain, block_lengths):
    nctx, nx = lax.axis_size("ctx"), lax.axis_size("head")
    heads_first = [jnp.moveaxis(a, 1, 0) for a in (queries, keys, values, out_grads)]
    big = (LOC, TOK, DH)
    dma = pltpu.SemaphoreType.DMA
    vmem = pltpu.VMEM
    out = jax.ShapeDtypeStruct(big, BF)
    any_spec = pl.BlockSpec(memory_space=pl.ANY)
    vmem_spec = pl.BlockSpec(memory_space=pltpu.VMEM)
    res = pl.pallas_call(
        functools.partial(body, nctx, nx),
        out_shape=(out, out, out),
        in_specs=[pl.BlockSpec(memory_space=pltpu.HBM)] * 7,
        out_specs=(vmem_spec, vmem_spec, vmem_spec),
        scratch_shapes=[
            vmem((LOC, DH), F32), vmem((LOC, DH), F32), vmem((1, block_lengths.shape[0]), jnp.int32),
            vmem(big, BF), vmem(big, BF), vmem((LOC, CUT, DH), BF), vmem((LOC, CUT, DH), BF), vmem(big, BF), vmem(big, BF),
            vmem((HALF, SPAN, DH), BF), vmem((HALF, SPAN, DH), BF),
            vmem((HALF, ROWS_Q, DH), BF), vmem((HALF, ROWS_Q, DH), BF),
            vmem((LOC, 2, CUT, DH), BF), vmem((HALF, 2, CUT, DH), BF),
            vmem((TOK, DH), F32), vmem((TOK, DH), F32),
            vmem((8, TOK), F32), vmem((nx - 1, 8, TOK), F32),
            vmem((NQ, WIN, QT), F32), vmem((NQ, 8, QT), F32), vmem((2, WIN, QT), F32), vmem((2, WIN, QT), F32),
            vmem((DH, SPAN), BF), vmem((SPAN, DH), F32), vmem((SPAN, DH), F32),
            vmem((SPAN, DH), F32), vmem((ROWS_Q, DH), F32), vmem((8, TOK), F32), vmem((nx - 1, 8, TOK), F32),
            vmem((8, TOK), F32), vmem((5, 8, TOK), F32),
            vmem((8, TOK), F32), vmem((3, 8, TOK), F32),
            vmem((HALF, 2, SPAN, DH), BF), vmem((HALF, ROWS_Q, DH), BF), vmem((HALF, 2, CUT, DH), BF),
            vmem((2,) + big, BF), vmem((2, LOC, CUT, DH), BF), vmem((2, LOC, CUT, DH), BF), vmem((HALF, 2, TOK, DH), BF), vmem((HALF, TOK, DH), BF),
            vmem(big, F32), vmem(big, F32),
            dma((11,)),
            dma((2, HALF, 2)), dma((2, HALF, 2)), dma((2, HALF, 2)), dma((2, HALF)),
            dma((4,)), dma((4,)), dma((2, 3)), dma((2, 3)),
            dma((HALF, 3)), dma((HALF, 2, 2)), dma((HALF,)), dma((HALF, 2)),
            dma((2, HALF)), dma((2, HALF)), dma((4,)), dma((5,)), dma((4,)), dma((3,)),
            dma((2, HALF, 2)), dma((2, HALF)), dma((HALF,)), dma((HALF, 2)),
        ],
        compiler_params=pltpu.CompilerParams(
            collective_id=0, has_side_effects=True, vmem_limit_bytes=52 << 20
        ),
    )(*heads_first, query_gain, key_gain, block_lengths.reshape(1, -1))
    return tuple(jnp.moveaxis(a, 0, 1) for a in res)


def solution(mesh):
    placed = (
        P("ctx", "head", None),
        P("ctx", "head", None),
        P("ctx", "head", None),
        P("ctx", "head", None),
        P("head", None),
        P("head", None),
        P(),
    )
    return jax.shard_map(
        local,
        mesh=mesh,
        in_specs=placed,
        out_specs=(P("ctx", "head", None), P("ctx", "head", None), P("ctx", "head", None)),
        check_vma=False,
    )
```
